128 devices in a mesh: grp: 2 (over y_hi), ep: 32 (over x, y_lo, z), tp: 2 (over core).
Axes of the slice: x: 4, y: 4 (y_hi: 2, y_lo: 2; y = y_hi * 2 + y_lo), z: 4, core: 2. Of those that a mesh axis runs over, the one named last changes fastest.
Arguments:
- tokens: bfloat16 [1024, 4096], P(('grp', 'ep', 'tp')), may hold values from -6 to 6
- teacher_gain: float32 [4096], replicated, may hold values from 0.1 to 1.9
- student_gain: float32 [4096], replicated, may hold values from 0.1 to 1.9
- expert_ids: int32 [1024, 8], P(('grp', 'ep', 'tp')), may hold values from 0 to 63, all different within a row; in each aligned block of 8 rows (0 to 7, 8 to 15, ...) at most 2 rows name the same one
- route_weights: float32 [1024, 8], P(('grp', 'ep', 'tp')), may hold values from 0.05 to 0.5
- expert_gate: bfloat16 [64, 4096, 768], P(('grp', 'ep'), None, 'tp'), may hold values from -0.09375 to 0.09375
- expert_up: bfloat16 [64, 4096, 768], P(('grp', 'ep'), None, 'tp'), may hold values from -0.09375 to 0.09375
- expert_down: bfloat16 [64, 768, 4096], P(('grp', 'ep'), 'tp'), may hold values from -0.21875 to 0.21875
- student_gate: bfloat16 [4096, 14336], P(None, ('ep', 'tp')), may hold values from -0.09375 to 0.09375
- student_up: bfloat16 [4096, 14336], P(None, ('ep', 'tp')), may hold values from -0.09375 to 0.09375
- student_down: bfloat16 [14336, 4096], P(('ep', 'tp')), may hold values from -0.046875 to 0.046875
Outputs:
- gate_grad: bfloat16 [4096, 14336], P(None, ('ep', 'tp'))
- up_grad: bfloat16 [4096, 14336], P(None, ('ep', 'tp'))
- down_grad: bfloat16 [14336, 4096], P(('ep', 'tp'))
The draws below stay inside these ranges and needn't reach their ends.
Inputs may be any that keep to these rules, and one draw needn't show every extreme that they name: `expert_ids`: each token names 8 different experts. The tokens of one device name one expert at most 2 times, and in every draw some device names some expert exactly 2 times.
All inputs are finite; a program needn't handle non-finite values.
Results may differ from the reference program's by a relative error of at most 0.011.
Values may be sent and summed in bfloat16 or wider, within the bound.
A program may use at most 128 MiB of HBM per device.

```python
import math
import jax
import jax.numpy as jnp
import numpy as np
from jax import lax

D = 4096
FFE = 768
FS = 14336
TOP = 8
TOK_DEV = 8
EXPERTS = 64
CAP = 2
TOKENS = 1024
N_GRP = 2
N_EP = 32
N_TP = 2


def level_of(key, dims, split, low, largest):
    loudness, own = 1.0, jax.random.fold_in(key, 6)
    for dim, blocks in split:
        steps = jnp.exp(jax.random.uniform(jax.random.fold_in(own, dim), (blocks,), jnp.float32, low / len(split), largest / len(split)))
        loudness = loudness * jnp.repeat(steps, dims[dim] // blocks).reshape([-1 if axis == dim else 1 for axis in range(len(dims))])
    return loudness


def deal_out(rng, own, number, rows, number_of, top, limit, lean):
    order = jax.random.permutation(rng, number_of)
    heavy_load, common = load_shares(number_of, rows * top, limit, lean, True), load_shares(number_of, rows * top, limit, lean, False)
    places = jnp.arange(number_of)

    def named(tallies, rotation):
        used = int((tallies > 0).sum())
        fixed = max(1, used // 4)
        shifted = fixed + (places - fixed + rotation * (used - fixed)) % max(1, number_of - fixed)
        return jnp.zeros((number_of,), jnp.int32).at[order[jnp.where(places < fixed, places, shifted)]].set(jnp.asarray(tallies, jnp.int32))

    tallies = jnp.where(number % 4 == 0, named(heavy_load, number // 4), named(common, number - number // 4 - 1))
    mixed = jax.random.permutation(jax.random.fold_in(own, 3), number_of)
    giver, receiver = mixed[0:number_of // 2 * 2:2], mixed[1:number_of // 2 * 2:2]
    room = jnp.minimum(tallies[giver] - 1, limit - tallies[receiver]) // 2
    room = jnp.where((giver == order[0]) | (receiver == order[0]) | (tallies[receiver] == 0), 0, jnp.maximum(room, 0))
    shifted = jax.random.randint(jax.random.fold_in(own, 4), (number_of // 2,), 0, 1 << 20) % (room + 1)
    tallies = tallies.at[giver].add(-shifted).at[receiver].add(shifted)
    items = jnp.searchsorted(jnp.cumsum(tallies), jnp.arange(rows * top), side="right").astype(jnp.int32)
    grid = items.reshape(top, rows).T
    grid = grid[jax.random.permutation(jax.random.fold_in(own, 1), rows)]
    rotation = jax.random.randint(jax.random.fold_in(own, 2), (rows, 1), 0, top)
    return jnp.take_along_axis(grid, (jnp.arange(top)[None, :] + rotation) % top, axis=1)


def load_shares(count, total, most, lean, full):
    portions = [(1 << 20) // math.isqrt(grade ** lean) + 1 for grade in range(1, count + 1)]
    largest = most if full else min(most, max(-(-total // count), total * portions[0] // sum(portions)))
    least = 1 if total - largest >= count - 1 else 0
    counts, surplus = [largest] + [least] * (count - 1), total - largest - least * (count - 1)
    while surplus > 0:
        free = [i for i in range(1, count) if counts[i] < largest] or [i for i in range(1, count) if counts[i] < most]
        mass, left = sum([portions[i] for i in free]), surplus
        for i in free:
            more = min(most - counts[i], max(1, left * portions[i] // mass), surplus)
            counts[i] = counts[i] + more
            surplus = surplus - more
    return np.array(counts)


def scatter_about(rng, dims, deviation, most, shards=(), kind=jnp.bfloat16):
    values = deviation * jax.random.normal(rng, dims, jnp.float32)
    if shards:
        values = values * level_of(rng, dims, shards, -0.22, 0.18)
    return jnp.clip(values, -most, most).astype(kind)


def setup_inputs(seed: int = 0) -> dict:
    key_list = jax.random.split(jax.random.key(seed), 12)
    tokens = scatter_about(key_list[0], (TOKENS, D), 1.0, 6.0, ((0, 128),))
    teacher_gain = jnp.clip(1.0 + 0.18 * jax.random.normal(key_list[1], (D,), jnp.float32), 0.1, 1.9)
    student_gain = jnp.clip(1.0 + 0.18 * jax.random.normal(key_list[2], (D,), jnp.float32), 0.1, 1.9)
    expert_ids_keys = jax.random.split(jax.random.fold_in(key_list[3], 1), TOKENS // TOK_DEV)
    expert_ids_turns = jax.random.permutation(jax.random.fold_in(key_list[3], 3), TOKENS // TOK_DEV)
    expert_ids = jax.vmap(lambda own, number: deal_out(jax.random.fold_in(key_list[3], 2), own, number, TOK_DEV, EXPERTS, TOP, CAP, 2))(expert_ids_keys, expert_ids_turns).reshape((TOKENS, TOP))
    route_weights = jnp.clip(jnp.exp(math.log(0.5) - 2.3025851 * jax.random.uniform(key_list[4], (TOKENS, TOP), jnp.float32) ** level_of(key_list[4], (TOKENS, TOP), ((0, 128),), -0.2, 0.2)), 0.05, 0.5)
    expert_gate = scatter_about(key_list[5], (EXPERTS, D, FFE), D ** -0.5, 0.09375, ((0, 64), (2, 2)))
    expert_up = scatter_about(key_list[6], (EXPERTS, D, FFE), D ** -0.5, 0.09375, ((0, 64), (2, 2)))
    expert_down = scatter_about(key_list[7], (EXPERTS, FFE, D), FFE ** -0.5, 0.21875, ((0, 64), (1, 2)))
    student_gate = scatter_about(key_list[8], (D, FS), D ** -0.5, 0.09375, ((1, 64),))
    student_up = scatter_about(key_list[9], (D, FS), D ** -0.5, 0.09375, ((1, 64),))
    student_down = scatter_about(key_list[10], (FS, D), FS ** -0.5, 0.046875, ((0, 64),))
    return dict(tokens=tokens, teacher_gain=teacher_gain, student_gain=student_gain, expert_ids=expert_ids, route_weights=route_weights, expert_gate=expert_gate, expert_up=expert_up, expert_down=expert_down, student_gate=student_gate, student_up=student_up, student_down=student_down)


EPSILON = 1e-06

def normalize(values, gain):
    wide = values.astype(jnp.float32)
    scaled = wide * lax.rsqrt(lax.optimization_barrier(jnp.mean(wide * wide, axis=-1, keepdims=True)) + EPSILON)
    return (scaled * gain).astype(jnp.bfloat16)

def reference(tokens, teacher_gain, student_gain, expert_ids, route_weights, expert_gate, expert_up, expert_down, student_gate, student_up, student_down):
    most_rows = N_GRP * N_EP * N_TP * CAP
    lane_width = FFE // N_TP
    teacher_in = normalize(tokens, teacher_gain)
    flat_ids = expert_ids.reshape(-1)
    flat_weights = route_weights.reshape(-1)

    def visit(total, inputs):
        number, gate_w, up_w, down_w = inputs
        chosen = flat_ids == number
        hit_count = jnp.sum(chosen.astype(jnp.int32))
        where = jnp.nonzero(chosen, size=most_rows, fill_value=0)[0].astype(jnp.int32)
        live = (jnp.arange(most_rows, dtype=jnp.int32) < hit_count).astype(jnp.float32)
        owner = (where // TOP).astype(jnp.int32)
        rows = teacher_in[owner]
        gate_pre = jnp.dot(rows, gate_w, preferred_element_type=jnp.float32)
        up_pre = jnp.dot(rows, up_w, preferred_element_type=jnp.float32)
        hidden = (jax.nn.silu(gate_pre) * up_pre).astype(jnp.bfloat16)
        summed = jnp.zeros((most_rows, D), jnp.float32)
        for lane in range(N_TP):
            piece = jnp.dot(hidden[:, lane * lane_width:(lane + 1) * lane_width], down_w[lane * lane_width:(lane + 1) * lane_width], preferred_element_type=jnp.float32)
            summed = summed + lax.optimization_barrier(piece.astype(jnp.bfloat16)).astype(jnp.float32)
        slots = lax.optimization_barrier(summed.astype(jnp.bfloat16)).astype(jnp.float32)
        weight = flat_weights[where] * live
        return (total.at[owner].add(slots * weight[:, None]), None)
    target, _ = lax.scan(visit, jnp.zeros((TOKENS, D), jnp.float32), (jnp.arange(EXPERTS, dtype=jnp.int32), expert_gate, expert_up, expert_down))
    student_in = normalize(tokens, student_gain)
    gate_pre = jnp.dot(student_in, student_gate, preferred_element_type=jnp.float32)
    up_pre = jnp.dot(student_in, student_up, preferred_element_type=jnp.float32)
    sigma = jax.nn.sigmoid(gate_pre)
    active = gate_pre * sigma
    hidden = (active * up_pre).astype(jnp.bfloat16)
    output = jnp.dot(hidden, student_down, preferred_element_type=jnp.float32)
    grad_out = ((output - target) * (1.0 / math.sqrt(TOKENS))).astype(jnp.bfloat16)
    grad_hidden = jnp.dot(grad_out, student_down.T, preferred_element_type=jnp.float32)
    grad_gate_pre = (grad_hidden * up_pre * sigma * (1.0 + gate_pre * (1.0 - sigma))).astype(jnp.bfloat16)
    grad_up_pre = (grad_hidden * active).astype(jnp.bfloat16)
    shard_rows = TOKENS // N_GRP
    gate_sum = jnp.zeros((D, FS), jnp.float32)
    up_sum = jnp.zeros((D, FS), jnp.float32)
    down_sum = jnp.zeros((FS, D), jnp.float32)
    for group in range(N_GRP):
        first = group * shard_rows
        last = first + shard_rows
        gate_term = jnp.dot(student_in[first:last].T, grad_gate_pre[first:last], preferred_element_type=jnp.float32)
        up_term = jnp.dot(student_in[first:last].T, grad_up_pre[first:last], preferred_element_type=jnp.float32)
        down_term = jnp.dot(hidden[first:last].T, grad_out[first:last], preferred_element_type=jnp.float32)
        gate_sum = gate_sum + lax.optimization_barrier(gate_term.astype(jnp.bfloat16)).astype(jnp.float32)
        up_sum = up_sum + lax.optimization_barrier(up_term.astype(jnp.bfloat16)).astype(jnp.float32)
        down_sum = down_sum + lax.optimization_barrier(down_term.astype(jnp.bfloat16)).astype(jnp.float32)
    return (gate_sum.astype(jnp.bfloat16), up_sum.astype(jnp.bfloat16), down_sum.astype(jnp.bfloat16))
```

```python
import functools
import math

import jax
import jax.numpy as jnp
from jax import lax
from jax.experimental import pallas as pl
from jax.experimental.pallas import tpu as pltpu
from jax.sharding import PartitionSpec as P

EPSILON = 1e-06
D = 4096
HALF = 2048
META = 128
WIDE = HALF + META
TOKENS = 1024
FE = 384
FU = 224
OWN = 112
MESH = pl.DeviceIdType.MESH
ORDERS = ((0, 1, 2), (1, 2, 0), (2, 0, 1))


def parts_of(width):
    lanes = width // 128
    cuts = [0, -(-lanes // 3), -(-lanes // 3) + -(-(lanes - -(-lanes // 3)) // 2), lanes]
    parts = []
    for p in range(3):
        low, high = cuts[p], cuts[p + 1]
        middle = low + (high - low + 1) // 2
        parts.append((low * 128, middle * 128, high * 128))
    return parts


class Place:
    def __init__(self):
        grp, ep, self.core = lax.axis_index("grp"), lax.axis_index("ep"), lax.axis_index("tp")
        self.at = (ep // 8, grp * 2 + (ep // 4) % 2, ep % 4)
        self.sibling = self.device(self.at, 1 - self.core)

    def device(self, at, core):
        x, y, z = at
        return (y // 2, (x * 2 + y % 2) * 4 + z, core)

    def along(self, dim, step):
        return (self.at[dim] + step + 4) % 4

    def neighbour(self, dim, step):
        at = list(self.at)
        at[dim] = self.along(dim, step)
        return self.device(at, self.core)

    def everyone(self):
        return [self.neighbour(dim, step) for dim in range(3) for step in (1, -1)] + [self.sibling]

    def group(self, order, phase, pos):
        index = [None] * 3
        for j, dim in enumerate(order):
            index[dim] = slice(None) if j < phase else (pos if j == phase else self.at[dim])
        return tuple(index)


def greet(place):
    barrier = pltpu.get_barrier_semaphore()
    friends = place.everyone()
    for device in friends:
        pl.semaphore_signal(barrier, inc=1, device_id=device, device_id_type=MESH)
    pl.semaphore_wait(barrier, len(friends))


def remote(src, dst, send, recv, device):
    return pltpu.make_async_remote_copy(
        src_ref=src, dst_ref=dst, send_sem=send, recv_sem=recv, device_id=device, device_id_type=MESH
    )


def gather(place, buf, width, send, recv, core_send, core_recv):
    parts = parts_of(width)
    core = place.core
    started = []

    def copy(p, phase, way, item, pos, cols):
        order = ORDERS[p]
        view = buf.at[(core,) + place.group(order, phase, pos) + (slice(None), pl.ds(cols[0], cols[1] - cols[0]))]
        return remote(
            view, view, send.at[p, phase, way, item], recv.at[p, phase, way, item],
            place.neighbour(order[phase], 1 if way == 0 else -1),
        )

    def across(p, item, pos, cols, plane):
        view = buf.at[(plane,) + place.group(ORDERS[p], 2, pos) + (slice(None), pl.ds(cols[0], cols[1] - cols[0]))]
        return remote(view, view, core_send.at[p, item], core_recv.at[p, item], place.sibling)

    def go(c):
        c.start()
        started.append(c)

    for phase in range(3):
        for p in range(3):
            low, mid, high = parts[p]
            halves = ((low, mid), (mid, high))
            me = place.at[ORDERS[p][phase]]
            for item in range(2):
                for way in range(2):
                    go(copy(p, phase, way, item, me, halves[item if way == 0 else 1 - item]))
            if phase == 2:
                go(across(p, 0, me, (low, high), core))
        for p in range(3):
            low, mid, high = parts[p]
            halves = ((low, mid), (mid, high))
            dim = ORDERS[p][phase]
            for way in range(2):
                pos = place.along(dim, -1 if way == 0 else 1)
                copy(p, phase, way, 0, pos, halves[way]).wait_recv()
                go(copy(p, phase, way, 2, pos, halves[way]))
        for p in range(3):
            low, mid, high = parts[p]
            halves = ((low, mid), (mid, high))
            dim = ORDERS[p][phase]
            for way in range(2):
                pos = place.along(dim, -1 if way == 0 else 1)
                copy(p, phase, way, 1, pos, halves[1 - way]).wait_recv()
                if phase == 2:
                    go(across(p, 1 + way, pos, (low, high), core))
        for p in range(3):
            low, mid, high = parts[p]
            halves = ((low, mid), (mid, high))
            dim = ORDERS[p][phase]
            far = place.along(dim, 2)
            for way in range(2):
                copy(p, phase, way, 2, far, halves[way]).wait_recv()
                if phase == 2:
                    go(across(p, 3 + way, far, halves[way], core))
    for p in range(3):
        low, mid, high = parts[p]
        dim = ORDERS[p][2]
        across(p, 0, place.at[dim], (low, high), 1 - core).wait_recv()
        across(p, 1, place.along(dim, -1), (low, high), 1 - core).wait_recv()
        across(p, 2, place.along(dim, 1), (low, high), 1 - core).wait_recv()
        across(p, 3, place.along(dim, 2), (low, mid), 1 - core).wait_recv()
        across(p, 4, place.along(dim, 2), (mid, high), 1 - core).wait_recv()
    for c in started:
        c.wait_send()


GATHER_SEMS = [
    pltpu.SemaphoreType.DMA((3, 3, 2, 3)),
    pltpu.SemaphoreType.DMA((3, 3, 2, 3)),
    pltpu.SemaphoreType.DMA((3, 5)),
    pltpu.SemaphoreType.DMA((3, 5)),
]


def gather_kernel(rows_ref, buf, other, block, local_sem, pair_send, pair_recv, send, recv, core_send, core_recv):
    place = Place()
    core = place.core
    greet(place)
    pair = remote(rows_ref.at[1 - core], other, pair_send, pair_recv, place.sibling)
    pair.start()
    pair.wait()
    mine, theirs = rows_ref[core], other[...]
    first = jnp.where(core == 0, mine, theirs)
    second = jnp.where(core == 0, theirs, mine)
    block[...] = jnp.concatenate([first, second], axis=0).astype(jnp.bfloat16)
    x, y, z = place.at
    put = pltpu.make_async_copy(block, buf.at[core, x, y, z], local_sem)
    put.start()
    put.wait()
    gather(place, buf, WIDE, send, recv, core_send, core_recv)


def gather_rows(rows):
    return pl.pallas_call(
        gather_kernel,
        out_shape=jax.ShapeDtypeStruct((2, 4, 4, 4, 16, WIDE), jnp.bfloat16),
        in_specs=[pl.BlockSpec(memory_space=pltpu.VMEM)],
        out_specs=pl.BlockSpec(memory_space=pl.ANY),
        scratch_shapes=[
            pltpu.VMEM((8, WIDE), jnp.float32),
            pltpu.VMEM((16, WIDE), jnp.bfloat16),
            pltpu.SemaphoreType.DMA,
            pltpu.SemaphoreType.DMA,
            pltpu.SemaphoreType.DMA,
        ]
        + GATHER_SEMS,
        compiler_params=pltpu.CompilerParams(collective_id=0, has_side_effects=True),
        name="gather_rows",
    )(rows)


RED_PARTS = parts_of(HALF)


def reduce_kernel(
    hid_ref, down_ref, buf, total, pair_buf, block, *rest
):
    recv_bufs = rest[:18]
    local_sem, pair_send, pair_recv, red_send, red_recv, send, recv, core_send, core_recv = rest[18:]
    place = Place()
    core = place.core
    greet(place)
    tile = 256
    started = []

    def multiply(plane):
        @pl.loop(0, HALF // tile)
        def _(t):
            first = pl.multiple_of(t * tile, tile)
            weights = down_ref[plane, :, pl.ds(first, tile)]
            for x in range(4):
                product = jnp.dot(hid_ref[pl.ds(x * 256, 256), :], weights, preferred_element_type=jnp.float32)
                total[plane, x, :, :, :, pl.ds(first, tile)] = product.astype(jnp.bfloat16).reshape(4, 4, 16, tile)

    def pair(part, plane):
        low, _, high = RED_PARTS[part]
        cols = pl.ds(low, high - low)
        return remote(
            total.at[plane, :, :, :, :, cols], pair_buf.at[:, :, :, :, cols],
            pair_send.at[part], pair_recv.at[part], place.sibling,
        )

    multiply(1 - core)
    for p in range(3):
        c = pair(p, 1 - core)
        c.start()
        started.append(c)
    multiply(core)

    def halves_of(p):
        low, mid, high = RED_PARTS[p]
        return ((low, mid), (mid, high))

    def view(p, phase, pos, cols):
        return total.at[(core,) + place.group(ORDERS[p], phase, pos) + (slice(None), pl.ds(cols[0], cols[1] - cols[0]))]

    def box(p, phase, way):
        return recv_bufs[(p * 3 + phase) * 2 + way]

    def spot(p, phase, way, item, cols):
        lead = (slice(None),) * phase
        if phase:
            return box(p, phase, way).at[(item,) + lead + (slice(None), pl.ds(0, cols[1] - cols[0]))]
        return box(p, phase, way).at[item, :, pl.ds(0, cols[1] - cols[0])]

    def send_part(p, phase, way, item, pos, cols):
        return remote(
            view(p, phase, pos, cols), spot(p, phase, way, item, cols),
            red_send.at[p, phase, way, item], red_recv.at[p, phase, way, item],
            place.neighbour(ORDERS[p][phase], 1 if way == 0 else -1),
        )

    def go(c):
        c.start()
        started.append(c)

    def add(p, phase, pos, cols, sources):
        lead = place.group(ORDERS[p], phase, pos)
        whole = [i for i, v in enumerate(lead) if isinstance(v, slice)]
        width = pl.ds(cols[0], cols[1] - cols[0])

        def step(number):
            index = list(lead)
            inner = []
            if len(whole) == 2:
                index[whole[0]], index[whole[1]] = number // 4, number % 4
            elif len(whole) == 1:
                index[whole[0]] = number
            inner = tuple(index[i] for i in whole)
            here = (core,) + tuple(index) + (slice(None), width)
            value = total[here].astype(jnp.float32)
            for source in sources:
                value = value + source[inner + (slice(None), slice(None))].astype(jnp.float32)
            return here, value

        if not whole:
            return step(0)[1]

        @pl.loop(0, 4 ** len(whole))
        def _(number):
            here, value = step(number)
            total[here] = value.astype(jnp.bfloat16)

    for phase in (2, 1, 0):
        for p in range(3):
            dim = ORDERS[p][phase]
            halves = halves_of(p)
            if phase == 2:
                pair(p, 1 - core).wait_recv()
                low, _, high = RED_PARTS[p]
                cols = pl.ds(low, high - low)

                @pl.loop(0, 64)
                def _(n):
                    at = (n // 16, (n // 4) % 4, n % 4, slice(None), cols)
                    total[(core,) + at] = (
                        total[(core,) + at].astype(jnp.float32) + pair_buf[at].astype(jnp.float32)
                    ).astype(jnp.bfloat16)

            for way in range(2):
                go(send_part(p, phase, way, 0, place.along(dim, 2), halves[way]))
            for way in range(2):
                go(send_part(p, phase, way, 1, place.along(dim, 1 if way == 0 else -1), halves[1 - way]))
        for p in range(3):
            dim = ORDERS[p][phase]
            halves = halves_of(p)
            for way in range(2):
                pos = place.along(dim, 1 if way == 0 else -1)
                send_part(p, phase, way, 0, pos, halves[way]).wait_recv()
                value = add(p, phase, pos, halves[way], [spot(p, phase, way, 0, halves[way])])
                if phase == 0:
                    view(p, 0, pos, halves[way])[...] = value.astype(jnp.bfloat16)
                go(send_part(p, phase, way, 2, pos, halves[way]))
        for p in range(3):
            dim = ORDERS[p][phase]
            halves = halves_of(p)
            me = place.at[dim]
            for half in range(2):
                send_part(p, phase, half, 2, me, halves[half]).wait_recv()
                send_part(p, phase, 1 - half, 1, me, halves[half]).wait_recv()
                value = add(
                    p, phase, me, halves[half],
                    [spot(p, phase, half, 2, halves[half]), spot(p, phase, 1 - half, 1, halves[half])],
                )
                if phase == 0:
                    width = pl.ds(halves[half][0], halves[half][1] - halves[half][0])
                    block[:, width] = (value * (1.0 / math.sqrt(TOKENS))).astype(jnp.bfloat16)
    x, y, z = place.at
    put = pltpu.make_async_copy(block, buf.at[core, x, y, z], local_sem)
    put.start()
    put.wait()
    gather(place, buf, HALF, send, recv, core_send, core_recv)
    for c in started:
        c.wait_send()


def reduce_and_gather(hid, down):
    boxes = []
    for p in range(3):
        low, mid, high = RED_PARTS[p]
        for phase in range(3):
            for way in range(2):
                boxes.append(pltpu.VMEM((3,) + (4,) * phase + (16, max(mid - low, high - mid)), jnp.bfloat16))
    return pl.pallas_call(
        reduce_kernel,
        out_shape=jax.ShapeDtypeStruct((2, 4, 4, 4, 16, HALF), jnp.bfloat16),
        in_specs=[pl.BlockSpec(memory_space=pltpu.VMEM)] * 2,
        out_specs=pl.BlockSpec(memory_space=pl.ANY),
        scratch_shapes=[
            pltpu.VMEM((2, 4, 4, 4, 16, HALF), jnp.bfloat16),
            pltpu.VMEM((4, 4, 4, 16, HALF), jnp.bfloat16),
            pltpu.VMEM((16, HALF), jnp.bfloat16),
        ]
        + boxes
        + [
            pltpu.SemaphoreType.DMA,
            pltpu.SemaphoreType.DMA((3,)),
            pltpu.SemaphoreType.DMA((3,)),
            pltpu.SemaphoreType.DMA((3, 3, 2, 3)),
            pltpu.SemaphoreType.DMA((3, 3, 2, 3)),
        ]
        + GATHER_SEMS,
        compiler_params=pltpu.CompilerParams(collective_id=1, has_side_effects=True, vmem_limit_bytes=48 << 20),
        name="reduce_and_gather",
    )(hid, down)


def body(
    tokens, teacher_gain, student_gain, expert_ids, route_weights,
    expert_gate, expert_up, expert_down, student_gate, student_up, student_down,
):
    grp = lax.axis_index("grp")
    expert = grp * 32 + lax.axis_index("ep")
    wide = tokens.astype(jnp.float32)
    scale = lax.rsqrt(jnp.mean(wide * wide, axis=-1, keepdims=True) + EPSILON)
    hits = expert_ids[:, :, None] == jnp.arange(64, dtype=jnp.int32)[None, None, :]
    table = jnp.sum(jnp.where(hits, route_weights[:, :, None], 0.0), axis=1)
    meta = jnp.concatenate([table, jnp.broadcast_to(scale, (8, 64))], axis=1)
    meta_high = meta.astype(jnp.bfloat16).astype(jnp.float32)
    meta_low = (meta - meta_high).astype(jnp.bfloat16).astype(jnp.float32)
    rows = jnp.stack(
        [
            jnp.concatenate([wide[:, :HALF], meta_high], axis=1),
            jnp.concatenate([wide[:, HALF:], meta_low], axis=1),
        ]
    )
    gathered = gather_rows(rows).reshape(2, TOKENS, WIDE)

    def scaled(weights, gain):
        value = (weights.astype(jnp.float32) * gain[:, None]).astype(jnp.bfloat16)
        return jnp.pad(value.reshape(2, HALF, -1), ((0, 0), (0, META), (0, 0)))

    facts = gathered[0, :, HALF:].astype(jnp.float32) + gathered[1, :, HALF:].astype(jnp.float32)
    row_scale = facts[:, 64:65]
    weight = lax.dynamic_slice_in_dim(facts, expert, 1, axis=1)

    def forward(weights, gain):
        pads = scaled(weights, gain)
        return row_scale * (
            jnp.dot(gathered[0], pads[0], preferred_element_type=jnp.float32)
            + jnp.dot(gathered[1], pads[1], preferred_element_type=jnp.float32)
        )

    teacher_gate = forward(expert_gate[0], teacher_gain)
    teacher_up = forward(expert_up[0], teacher_gain)
    teacher_hidden = (jax.nn.silu(teacher_gate) * teacher_up * -weight).astype(jnp.bfloat16)
    gate_pre = forward(student_gate, student_gain)
    up_pre = forward(student_up, student_gain)
    sigma = jax.nn.sigmoid(gate_pre)
    active = gate_pre * sigma
    hidden = (active * up_pre).astype(jnp.bfloat16)
    own = jnp.where(grp == 0, hidden[:, :OWN], hidden[:, OWN:])
    hid = jnp.concatenate([teacher_hidden, jnp.pad(own, ((0, 0), (0, 128 - OWN)))], axis=1)
    own_down = jnp.where(grp == 0, student_down[:OWN], student_down[OWN:])
    down = jnp.concatenate([expert_down[0], jnp.pad(own_down, ((0, 128 - OWN), (0, 0)))], axis=0)
    down = jnp.stack([down[:, :HALF], down[:, HALF:]])
    grad_out = reduce_and_gather(hid, down).reshape(2, TOKENS, HALF)
    grad_hidden = sum(
        lax.dot_general(
            grad_out[h], student_down[:, h * HALF:(h + 1) * HALF], (((1,), (1,)), ((), ())),
            preferred_element_type=jnp.float32,
        )
        for h in range(2)
    )
    grad_gate_pre = (row_scale * grad_hidden * up_pre * sigma * (1.0 + gate_pre * (1.0 - sigma))).astype(jnp.bfloat16)
    grad_up_pre = (row_scale * grad_hidden * active).astype(jnp.bfloat16)

    def input_grad(pre):
        wide = [
            lax.dot_general(gathered[h], pre, (((0,), (0,)), ((), ())), preferred_element_type=jnp.float32)[:HALF]
            for h in range(2)
        ]
        return (jnp.concatenate(wide) * student_gain[:, None]).astype(jnp.bfloat16)

    down_grad = jnp.concatenate(
        [
            lax.dot_general(hidden, grad_out[h], (((0,), (0,)), ((), ())), preferred_element_type=jnp.float32)
            for h in range(2)
        ],
        axis=1,
    ).astype(jnp.bfloat16)
    return input_grad(grad_gate_pre), input_grad(grad_up_pre), down_grad


def solution(mesh):
    everywhere = ("grp", "ep", "tp")
    in_specs = (
        P(everywhere, None),
        P(),
        P(),
        P(everywhere, None),
        P(everywhere, None),
        P(("grp", "ep"), None, "tp"),
        P(("grp", "ep"), None, "tp"),
        P(("grp", "ep"), "tp", None),
        P(None, ("ep", "tp")),
        P(None, ("ep", "tp")),
        P(("ep", "tp"), None),
    )
    out_specs = (P(None, ("ep", "tp")), P(None, ("ep", "tp")), P(("ep", "tp"), None))
    return jax.shard_map(body, mesh=mesh, in_specs=in_specs, out_specs=out_specs, check_vma=False)
```

```python
import math

import jax
import jax.numpy as jnp
from jax import lax
from jax.experimental import pallas as pl
from jax.experimental.pallas import tpu as pltpu
from jax.sharding import PartitionSpec as P

EPSILON = 1e-06
D = 4096
HALF = 2048
META = 128
WIDE = HALF + META
TOKENS = 1024
FE = 384
FU = 224
OWN = 112
MESH = pl.DeviceIdType.MESH
ORDERS = ((0, 1, 2), (1, 2, 0), (2, 0, 1))
ROWS_OUT = (0, -1, 1, 2)
ROWS_IN = (2, 1, -1, 0)
STEPS = (1, -1, 2)
IN_PARTS = ((0, 384, 768), (768, 1152, 1536), (1536, 1920, WIDE))
OUT_PARTS = ((0, 384, 768), (768, 1152, 1408), (1408, 1792, HALF))


class Place:
    def __init__(self):
        self.grp, ep, self.core = lax.axis_index("grp"), lax.axis_index("ep"), lax.axis_index("tp")
        self.expert = self.grp * 32 + ep
        self.at = (ep // 8, self.grp * 2 + (ep // 4) % 2, ep % 4)
        self.sibling = self.device(self.at, 1 - self.core)

    def device(self, at, core):
        x, y, z = at
        return (y // 2, (x * 2 + y % 2) * 4 + z, core)

    def along(self, dim, step):
        return (self.at[dim] + step + 4) % 4

    def neighbour(self, dim, step):
        at = list(self.at)
        at[dim] = self.along(dim, step)
        return self.device(at, self.core)

    def block(self, p, step):
        index = list(self.at)
        index[ORDERS[p][0]] = self.along(ORDERS[p][0], step)
        return tuple(index)

    def row(self, p, second, third):
        a, b, d = ORDERS[p]
        index = [None] * 3
        index[a], index[b], index[d] = slice(None), self.along(b, second), self.along(d, third)
        return tuple(index)

    def group(self, p, third):
        a, b, d = ORDERS[p]
        index = [None] * 3
        index[a], index[b], index[d] = slice(None), slice(None), self.along(d, third)
        return tuple(index)


def greet(place):
    friends = [place.neighbour(dim, step) for dim in range(3) for step in STEPS] + [place.sibling]
    barrier = pltpu.get_barrier_semaphore()
    for device in friends:
        pl.semaphore_signal(barrier, inc=1, device_id=device, device_id_type=MESH)
    pl.semaphore_wait(barrier, len(friends))


def remote(src, dst, send, recv, device):
    return pltpu.make_async_remote_copy(
        src_ref=src, dst_ref=dst, send_sem=send, recv_sem=recv, device_id=device, device_id_type=MESH
    )


GATHER_SEMS = [
    pltpu.SemaphoreType.DMA((2, 3, 3)),
    pltpu.SemaphoreType.DMA((2, 3, 3)),
    pltpu.SemaphoreType.DMA((2, 3, 4, 2)),
    pltpu.SemaphoreType.DMA((2, 3, 4, 2)),
    pltpu.SemaphoreType.DMA((2, 3, 4)),
]
REDUCE_SEMS = [
    pltpu.SemaphoreType.DMA((2, 3)),
    pltpu.SemaphoreType.DMA((2, 3, 4, 2, 3)),
    pltpu.SemaphoreType.DMA((2, 3, 3)),
    pltpu.SemaphoreType.DMA((2, 3, 3)),
]


class Gather:
    def __init__(self, place, buf, parts, sems):
        self.place, self.buf, self.parts = place, buf, parts
        self.block_sem, self.row_sem, self.near_sem, self.far_sem, self.across_sem = sems
        self.started = []

    def go(self, copy):
        copy.start()
        self.started.append(copy)

    def view(self, p, index, half=None, plane=None):
        low, mid, high = self.parts[p]
        if half is not None:
            low, high = ((low, mid), (mid, high))[half]
        plane = self.place.core if plane is None else plane
        return self.buf.at[(plane,) + index + (slice(None), pl.ds(low, high - low))]

    def copy(self, view, sem, spot, device):
        return remote(view, view, sem.at[(0,) + spot], sem.at[(1,) + spot], device)

    def block(self, p, i, step):
        view = self.view(p, self.place.block(p, step))
        return self.copy(view, self.block_sem, (p, i), self.place.neighbour(ORDERS[p][0], STEPS[i]))

    def row(self, p, i, step):
        view = self.view(p, self.place.row(p, step, 0))
        return self.copy(view, self.row_sem, (p, i), self.place.neighbour(ORDERS[p][1], STEPS[i]))

    def near(self, p, r, way, step):
        view = self.view(p, self.place.row(p, ROWS_OUT[r], step))
        return self.copy(view, self.near_sem, (p, r, way), self.place.neighbour(ORDERS[p][2], STEPS[way]))

    def far(self, p, r, way, step):
        view = self.view(p, self.place.row(p, ROWS_OUT[r], step), half=way)
        return self.copy(view, self.far_sem, (p, r, way), self.place.neighbour(ORDERS[p][2], STEPS[way]))

    def across(self, p, g, plane):
        view = self.view(p, self.place.group(p, ROWS_OUT[g]), plane=plane)
        return self.copy(view, self.across_sem, (p, g), self.place.sibling)

    def send_blocks(self):
        for i in range(3):
            for p in range(3):
                self.go(self.block(p, i, 0))

    def send_rows(self):
        for p in range(3):
            for i in range(3):
                self.block(p, i, -STEPS[i]).wait_recv()
            for i in range(3):
                self.go(self.row(p, i, 0))
        self.spread(0)

    def spread(self, r):
        for p in range(3):
            for way in range(2):
                self.go(self.near(p, r, way, 0))

    def take_row(self, r):
        i = {-1: 0, 1: 1, 2: 2}[ROWS_OUT[r]]
        for p in range(3):
            self.row(p, i, -STEPS[i]).wait_recv()
        self.spread(r)

    def pass_on(self, r):
        for p in range(3):
            for way in range(2):
                self.near(p, r, way, -STEPS[way]).wait_recv()
                self.go(self.far(p, r, way, -STEPS[way]))

    def take_far(self, r):
        for p in range(3):
            for way in range(2):
                self.far(p, r, way, 2).wait_recv()

    def cross(self, g):
        for p in range(3):
            self.go(self.across(p, g, self.place.core))

    def take_across(self, p, g):
        self.across(p, g, 1 - self.place.core).wait_recv()

    def finish(self):
        for copy in self.started:
            copy.wait_send()


class Reduce:
    def __init__(self, place, total, pair_buf, boxes, row_boxes, block_boxes, sems):
        self.place, self.total, self.pair_buf = place, total, pair_buf
        self.boxes, self.row_boxes, self.block_boxes = boxes, row_boxes, block_boxes
        self.pair_sem, self.ring_sem, self.row_sem, self.block_sem = sems
        self.started = []

    def go(self, copy):
        copy.start()
        self.started.append(copy)

    def halves(self, p):
        low, mid, high = OUT_PARTS[p]
        return ((low, mid - low), (mid, high - mid))

    def pair(self, p):
        low, _, high = OUT_PARTS[p]
        cols = pl.ds(low, high - low)
        return remote(
            self.total.at[1 - self.place.core, :, :, :, :, cols], self.pair_buf.at[:, :, :, :, cols],
            self.pair_sem.at[0, p], self.pair_sem.at[1, p], self.place.sibling,
        )

    def ring(self, p, r, way, item, step, half):
        low, width = self.halves(p)[half]
        view = self.total.at[
            (self.place.core,) + self.place.row(p, ROWS_IN[r], step) + (slice(None), pl.ds(low, width))
        ]
        return remote(
            view, self.boxes[p].at[way, item, r, :, :, pl.ds(0, width)],
            self.ring_sem.at[0, p, r, way, item], self.ring_sem.at[1, p, r, way, item],
            self.place.neighbour(ORDERS[p][2], STEPS[way]),
        )

    def row(self, p, i, step):
        low, _, high = OUT_PARTS[p]
        view = self.total.at[(self.place.core,) + self.place.row(p, step, 0) + (slice(None), pl.ds(low, high - low))]
        return remote(
            view, self.row_boxes.at[i, :, :, pl.ds(low, high - low)],
            self.row_sem.at[0, p, i], self.row_sem.at[1, p, i], self.place.neighbour(ORDERS[p][1], STEPS[i]),
        )

    def block(self, p, i, step):
        low, _, high = OUT_PARTS[p]
        view = self.total.at[(self.place.core,) + self.place.block(p, step) + (slice(None), pl.ds(low, high - low))]
        return remote(
            view, self.block_boxes.at[i, :, pl.ds(low, high - low)],
            self.block_sem.at[0, p, i], self.block_sem.at[1, p, i], self.place.neighbour(ORDERS[p][0], STEPS[i]),
        )

    def add(self, p, row, low, width, sources):
        a = ORDERS[p][0]
        cols = pl.ds(low, width)

        @pl.loop(0, 4)
        def _(n):
            index = list(row)
            index[a] = n
            here = (self.place.core,) + tuple(index) + (slice(None), cols)
            value = self.total[here].astype(jnp.float32)
            for source in sources:
                value = value + source[n].astype(jnp.float32)
            self.total[here] = value.astype(jnp.bfloat16)

    def start_part(self, p):
        for r in range(4):
            for way in range(2):
                self.go(self.ring(p, r, way, 0, 2, way))
            for way in range(2):
                self.go(self.ring(p, r, way, 1, STEPS[way], 1 - way))

    def pass_on(self, r):
        for p in range(3):
            for way in range(2):
                low, width = self.halves(p)[way]
                self.ring(p, r, way, 0, 0, way).wait_recv()
                self.add(
                    p, self.place.row(p, ROWS_IN[r], STEPS[way]), low, width,
                    [self.boxes[p].at[way, 0, r, :, :, pl.ds(0, width)]],
                )
                self.go(self.ring(p, r, way, 2, STEPS[way], way))

    def combine(self, r):
        for p in range(3):
            for half in range(2):
                low, width = self.halves(p)[half]
                self.ring(p, r, half, 2, 0, half).wait_recv()
                self.ring(p, r, 1 - half, 1, 0, half).wait_recv()
                self.add(
                    p, self.place.row(p, ROWS_IN[r], 0), low, width,
                    [
                        self.boxes[p].at[half, 2, r, :, :, pl.ds(0, width)],
                        self.boxes[p].at[1 - half, 1, r, :, :, pl.ds(0, width)],
                    ],
                )
            if ROWS_IN[r]:
                self.go(self.row(p, STEPS.index(ROWS_IN[r]), ROWS_IN[r]))

    def last_row(self):
        for p in range(3):
            low, _, high = OUT_PARTS[p]
            for i in range(3):
                self.row(p, i, 0).wait_recv()
            self.add(
                p, self.place.row(p, 0, 0), low, high - low,
                [self.row_boxes.at[i, :, :, pl.ds(low, high - low)] for i in range(3)],
            )
            for i in range(3):
                self.go(self.block(p, i, STEPS[i]))

    def last_block(self, buf):
        for p in range(3):
            low, _, high = OUT_PARTS[p]
            cols = pl.ds(low, high - low)
            for i in range(3):
                self.block(p, i, 0).wait_recv()
            here = (self.place.core,) + self.place.at + (slice(None), cols)
            value = self.total[here].astype(jnp.float32)
            for i in range(3):
                value = value + self.block_boxes[i, :, cols].astype(jnp.float32)
            buf[here] = (value * (1.0 / math.sqrt(TOKENS))).astype(jnp.bfloat16)

    def finish(self):
        for copy in self.started:
            copy.wait_send()


def gain_rows(gain_ref, number):
    return jnp.broadcast_to(gain_ref[pl.ds(number, 1), :], (128, 128)).T


def step_kernel(
    rows_ref, tgain_ref, sgain_ref, eg, eu, ed, sg, su, sd, gate_out, up_out, down_out,
    x_buf, g_buf, total, pair_buf, w_teacher, w_gate, w_up, down, s_down,
    acc_teacher, acc_gate, acc_up, grad_hidden, hid, hidden, other,
    box0, box1, box2, row_boxes, block_boxes, load_sem, store_sem, first_sem, *sems
):
    place = Place()
    core = place.core
    loads = []
    for q in range(4):
        cut = pl.ds(q * 1024, 1024)
        loads.append(
            [
                pltpu.make_async_copy(eg.at[cut], w_teacher.at[cut, pl.ds(0, FE)], load_sem.at[q, 0]),
                pltpu.make_async_copy(eu.at[cut], w_teacher.at[cut, pl.ds(FE, FE)], load_sem.at[q, 1]),
                pltpu.make_async_copy(sg.at[cut], w_gate.at[cut], load_sem.at[q, 2]),
                pltpu.make_async_copy(su.at[cut], w_up.at[cut], load_sem.at[q, 3]),
            ]
        )
    own_rows = pl.ds(pl.multiple_of(place.grp * OWN, 16), OWN)
    loads.append(
        [
            pltpu.make_async_copy(ed, down.at[pl.ds(0, FE)], load_sem.at[4, 0]),
            pltpu.make_async_copy(sd.at[own_rows], down.at[pl.ds(FE, OWN)], load_sem.at[4, 1]),
            pltpu.make_async_copy(sd, s_down, load_sem.at[4, 2]),
        ]
    )
    for bundle in loads:
        for load in bundle:
            load.start()
    down[FE + OWN:, :] = jnp.zeros((512 - FE - OWN, D), jnp.bfloat16)

    @pl.loop(0, 4)
    def _(x):
        for acc in (acc_teacher, acc_gate, acc_up, grad_hidden):
            acc[x] = jnp.zeros(acc.shape[1:], jnp.float32)

    greet(place)

    first = remote(rows_ref.at[1 - core], other, first_sem.at[0], first_sem.at[1], place.sibling)
    first.start()
    first.wait()
    mine, theirs = rows_ref[core], other[...]
    top = jnp.where(core == 0, mine, theirs)
    bottom = jnp.where(core == 0, theirs, mine)
    x_buf[(core,) + place.at] = jnp.concatenate([top, bottom], axis=0).astype(jnp.bfloat16)

    def scale(q):
        for load in loads[q]:
            load.wait()

        @pl.loop(q * 8, q * 8 + 8)
        def _(n):
            cut = pl.ds(pl.multiple_of(n * 128, 128), 128)
            gain = gain_rows(tgain_ref, n)
            for t in range(2 * FE // 128):
                cols = pl.ds(t * 128, 128)
                w_teacher[cut, cols] = (w_teacher[cut, cols].astype(jnp.float32) * gain).astype(jnp.bfloat16)
            gain = gain_rows(sgain_ref, n)
            gain = jnp.concatenate([gain, gain[:, :FU - 128]], axis=1)
            for w in (w_gate, w_up):
                w[cut] = (w[cut].astype(jnp.float32) * gain).astype(jnp.bfloat16)

    def forward(p, g):
        index = place.group(p, ROWS_OUT[g])
        low, _, high = IN_PARTS[p]
        high = min(high, HALF)
        lhs = [x_buf[(h,) + index + (slice(None), pl.ds(low, high - low))].reshape(256, high - low) for h in range(2)]

        def product(w, cols):
            return sum(
                jnp.dot(lhs[h], w[pl.ds(h * HALF + low, high - low), cols], preferred_element_type=jnp.float32)
                for h in range(2)
            )

        def put(acc, cols, value):
            here = index + (slice(None), cols)
            value = value.reshape(4, 4, 16, value.shape[-1])
            acc[here] = acc[here] + value

        @pl.loop(0, 2 * FE // 256)
        def _(t):
            cols = pl.ds(pl.multiple_of(t * 256, 256), 256)
            put(acc_teacher, cols, product(w_teacher, cols))

        put(acc_gate, slice(None), product(w_gate, slice(None)))
        put(acc_up, slice(None), product(w_up, slice(None)))

    ins = Gather(place, x_buf, IN_PARTS, sems[:5])
    ins.send_blocks()
    scale(0)
    ins.send_rows()
    scale(1)
    ins.take_row(1)
    ins.take_row(2)
    scale(2)
    ins.pass_on(0)
    ins.take_row(3)
    ins.cross(0)
    scale(3)
    ins.pass_on(1)
    for p in range(3):
        ins.take_across(p, 0)
        forward(p, 0)
    ins.pass_on(2)
    ins.pass_on(3)
    ins.cross(1)
    ins.cross(2)
    for g in (1, 2):
        for p in range(3):
            ins.take_across(p, g)
            forward(p, g)
        if g == 1:
            ins.take_far(0)
            ins.take_far(1)
    ins.take_far(2)
    ins.take_far(3)
    ins.cross(3)
    for p in range(3):
        ins.take_across(p, 3)
        forward(p, 3)
    for load in loads[4]:
        load.wait()

    lanes = lax.broadcasted_iota(jnp.int32, (256, META), 1)

    def facts(x):
        known = sum(x_buf[h, x, :, :, :, pl.ds(HALF, META)].astype(jnp.float32) for h in range(2)).reshape(256, META)
        row_scale = jnp.sum(jnp.where(lanes == 64, known, 0.0), axis=1, keepdims=True)
        weight = jnp.sum(jnp.where(lanes == place.expert, known, 0.0), axis=1, keepdims=True)
        return row_scale, weight

    @pl.loop(0, 4)
    def _(x):
        row_scale, weight = facts(x)
        gate = acc_teacher[x, :, :, :, pl.ds(0, FE)].reshape(256, FE) * row_scale
        up = acc_teacher[x, :, :, :, pl.ds(FE, FE)].reshape(256, FE) * row_scale
        value = gate * jax.nn.sigmoid(gate) * up * -weight
        hid[x, :, :, :, pl.ds(0, FE)] = value.astype(jnp.bfloat16).reshape(4, 4, 16, FE)
        gate = acc_gate[x].reshape(256, FU) * row_scale
        up = acc_up[x].reshape(256, FU) * row_scale
        acc_gate[x] = gate.reshape(4, 4, 16, FU)
        acc_up[x] = up.reshape(4, 4, 16, FU)
        value = gate * jax.nn.sigmoid(gate) * up
        hidden[x] = value.astype(jnp.bfloat16).reshape(4, 4, 16, FU)
        own = jnp.where(place.grp == 0, value[:, :OWN], value[:, OWN:])
        own = jnp.concatenate([own, jnp.zeros((256, 128 - OWN), jnp.float32)], axis=1)
        hid[x, :, :, :, pl.ds(FE, 128)] = own.astype(jnp.bfloat16).reshape(4, 4, 16, 128)

    red = Reduce(place, total, pair_buf, (box0, box1, box2), row_boxes, block_boxes, sems[5:9])

    def multiply(p, plane, added):
        low, _, high = OUT_PARTS[p]
        width = high - low
        cols = pl.ds(low, width)
        weights = pl.ds(pl.multiple_of(plane * HALF + low, 128), width)

        @pl.loop(0, 4)
        def _(x):
            value = jnp.dot(hid[x].reshape(256, 512), down[:, weights], preferred_element_type=jnp.float32)
            value = value.reshape(4, 4, 16, width)
            if added:
                value = value + pair_buf[x, :, :, :, cols].astype(jnp.float32)
            total[plane, x, :, :, :, cols] = value.astype(jnp.bfloat16)

    for p in range(3):
        multiply(p, 1 - core, False)
        red.go(red.pair(p))
    for p in range(3):
        red.pair(p).wait_recv()
        multiply(p, core, True)
        red.start_part(p)
    red.pass_on(0)
    red.pass_on(1)
    red.combine(0)
    red.pass_on(2)
    red.combine(1)
    red.pass_on(3)
    red.combine(2)
    red.combine(3)
    red.last_row()
    red.last_block(g_buf)

    def backward(p, g):
        index = place.group(p, ROWS_OUT[g])
        low, _, high = OUT_PARTS[p]
        width = high - low
        value = sum(
            lax.dot_general(
                g_buf[(h,) + index + (slice(None), pl.ds(low, width))].reshape(256, width),
                s_down[:, pl.ds(h * HALF + low, width)], (((1,), (1,)), ((), ())), preferred_element_type=jnp.float32,
            )
            for h in range(2)
        ).reshape(4, 4, 16, FU)
        grad_hidden[index] = grad_hidden[index] + value

    outs = Gather(place, g_buf, OUT_PARTS, sems[9:14])
    outs.send_blocks()
    outs.send_rows()
    outs.take_row(1)
    outs.take_row(2)
    outs.pass_on(0)
    outs.take_row(3)
    outs.cross(0)
    outs.pass_on(1)
    for p in range(3):
        outs.take_across(p, 0)
        backward(p, 0)
    outs.pass_on(2)
    outs.pass_on(3)
    outs.cross(1)
    outs.cross(2)
    for g in (1, 2):
        for p in range(3):
            outs.take_across(p, g)
            backward(p, g)
    for r in range(4):
        outs.take_far(r)
    outs.cross(3)
    for p in range(3):
        outs.take_across(p, 3)
        backward(p, 3)

    @pl.loop(0, 4)
    def _(x):
        row_scale, _ = facts(x)
        gate, up = acc_gate[x].reshape(256, FU), acc_up[x].reshape(256, FU)
        sigma = jax.nn.sigmoid(gate)
        grad = grad_hidden[x].reshape(256, FU) * row_scale
        gate_part = grad * up * sigma * (1.0 + gate * (1.0 - sigma))
        up_part = grad * gate * sigma
        hid[x, :, :, :, pl.ds(0, FU)] = gate_part.astype(jnp.bfloat16).reshape(4, 4, 16, FU)
        hid[x, :, :, :, pl.ds(256, FU)] = up_part.astype(jnp.bfloat16).reshape(4, 4, 16, FU)

    stores = []
    for h in range(2):

        @pl.loop(0, HALF // 256)
        def _(t):
            cols = pl.ds(pl.multiple_of(t * 256, 256), 256)
            rows = x_buf[h, :, :, :, :, cols].reshape(TOKENS, 256)
            value = lax.dot_general(
                rows, hid[...].reshape(TOKENS, 512), (((0,), (0,)), ((), ())), preferred_element_type=jnp.float32
            )
            gain = jnp.concatenate([gain_rows(sgain_ref, h * 16 + t * 2 + i) for i in range(2)], axis=0)
            gain = jnp.concatenate([gain, gain[:, :FU - 128]], axis=1)
            cut = pl.ds(pl.multiple_of(h * HALF + t * 256, 256), 256)
            w_gate[cut] = (value[:, :FU] * gain).astype(jnp.bfloat16)
            w_up[cut] = (value[:, 256:256 + FU] * gain).astype(jnp.bfloat16)

        cut = pl.ds(h * HALF, HALF)
        for i, (buf, out) in enumerate(((w_gate, gate_out), (w_up, up_out))):
            store = pltpu.make_async_copy(buf.at[cut], out.at[cut], store_sem.at[h, i])
            store.start()
            stores.append(store)
    for h in range(2):

        @pl.loop(0, HALF // 256)
        def _(t):
            cols = pl.ds(pl.multiple_of(t * 256, 256), 256)
            value = lax.dot_general(
                hidden[...].reshape(TOKENS, FU), g_buf[h, :, :, :, :, cols].reshape(TOKENS, 256),
                (((0,), (0,)), ((), ())), preferred_element_type=jnp.float32,
            )
            s_down[:, pl.ds(pl.multiple_of(h * HALF + t * 256, 256), 256)] = value.astype(jnp.bfloat16)

        cols = pl.ds(h * HALF, HALF)
        store = pltpu.make_async_copy(s_down.at[:, cols], down_out.at[:, cols], store_sem.at[h, 2])
        store.start()
        stores.append(store)
    ins.finish()
    red.finish()
    outs.finish()
    for store in stores:
        store.wait()


def step(rows, tgain, sgain, eg, eu, ed, sg, su, sd):
    bf16, f32 = jnp.bfloat16, jnp.float32
    vmem, hbm = pl.BlockSpec(memory_space=pltpu.VMEM), pl.BlockSpec(memory_space=pl.ANY)
    return pl.pallas_call(
        step_kernel,
        out_shape=(
            jax.ShapeDtypeStruct((D, FU), bf16),
            jax.ShapeDtypeStruct((D, FU), bf16),
            jax.ShapeDtypeStruct((FU, D), bf16),
        ),
        in_specs=[vmem] * 3 + [hbm] * 6,
        out_specs=[hbm] * 3,
        scratch_shapes=[
            pltpu.VMEM((2, 4, 4, 4, 16, WIDE), bf16),
            pltpu.VMEM((2, 4, 4, 4, 16, HALF), bf16),
            pltpu.VMEM((2, 4, 4, 4, 16, HALF), bf16),
            pltpu.VMEM((4, 4, 4, 16, HALF), bf16),
            pltpu.VMEM((D, 2 * FE), bf16),
            pltpu.VMEM((D, FU), bf16),
            pltpu.VMEM((D, FU), bf16),
            pltpu.VMEM((512, D), bf16),
            pltpu.VMEM((FU, D), bf16),
            pltpu.VMEM((4, 4, 4, 16, 2 * FE), f32),
            pltpu.VMEM((4, 4, 4, 16, FU), f32),
            pltpu.VMEM((4, 4, 4, 16, FU), f32),
            pltpu.VMEM((4, 4, 4, 16, FU), f32),
            pltpu.VMEM((4, 4, 4, 16, 512), bf16),
            pltpu.VMEM((4, 4, 4, 16, FU), bf16),
            pltpu.VMEM((8, WIDE), f32),
        ]
        + [pltpu.VMEM((2, 3, 4, 4, 16, 384), bf16)] * 3
        + [
            pltpu.VMEM((3, 4, 16, HALF), bf16),
            pltpu.VMEM((3, 16, HALF), bf16),
            pltpu.SemaphoreType.DMA((5, 4)),
            pltpu.SemaphoreType.DMA((2, 3)),
            pltpu.SemaphoreType.DMA((2,)),
        ]
        + GATHER_SEMS
        + REDUCE_SEMS
        + GATHER_SEMS,
        compiler_params=pltpu.CompilerParams(collective_id=0, has_side_effects=True, vmem_limit_bytes=63 << 20),
        name="distill",
    )(rows, tgain, sgain, eg, eu, ed, sg, su, sd)


def body(
    tokens, teacher_gain, student_gain, expert_ids, route_weights,
    expert_gate, expert_up, expert_down, student_gate, student_up, student_down,
):
    wide = tokens.astype(jnp.float32)
    scale = lax.rsqrt(jnp.mean(wide * wide, axis=-1, keepdims=True) + EPSILON)
    hits = expert_ids[:, :, None] == jnp.arange(64, dtype=jnp.int32)[None, None, :]
    table = jnp.sum(jnp.where(hits, route_weights[:, :, None], 0.0), axis=1)
    meta = jnp.concatenate([table, jnp.broadcast_to(scale, (8, 64))], axis=1)
    meta_high = lax.reduce_precision(meta, 8, 7)
    rows = jnp.stack(
        [
            jnp.concatenate([wide[:, :HALF], meta_high], axis=1),
            jnp.concatenate([wide[:, HALF:], meta - meta_high], axis=1),
        ]
    )
    return step(
        rows, teacher_gain.reshape(32, 128), student_gain.reshape(32, 128),
        expert_gate[0], expert_up[0], expert_down[0], student_gate, student_up, student_down,
    )


def solution(mesh):
    everywhere = ("grp", "ep", "tp")
    in_specs = (
        P(everywhere, None),
        P(),
        P(),
        P(everywhere, None),
        P(everywhere, None),
        P(("grp", "ep"), None, "tp"),
        P(("grp", "ep"), None, "tp"),
        P(("grp", "ep"), "tp", None),
        P(None, ("ep", "tp")),
        P(None, ("ep", "tp")),
        P(("ep", "tp"), None),
    )
    out_specs = (P(None, ("ep", "tp")), P(None, ("ep", "tp")), P(("ep", "tp"), None))
    return jax.shard_map(body, mesh=mesh, in_specs=in_specs, out_specs=out_specs, check_vma=False)
```

```python
import math

import jax
import jax.numpy as jnp
from jax import lax
from jax.experimental import pallas as pl
from jax.experimental.pallas import tpu as pltpu
from jax.sharding import PartitionSpec as P

EPSILON = 1e-06
D = 4096
HALF = 2048
META = 128
WIDE = HALF + META
TOKENS = 1024
FE = 384
FU = 224
OWN = 112
MESH = pl.DeviceIdType.MESH
ORDERS = ((0, 1, 2), (1, 2, 0), (2, 0, 1))
ROWS_OUT = (0, -1, 1, 2)
ROWS_IN = (2, 1, -1, 0)
STEPS = (1, -1, 2)
IN_PARTS = ((0, 384, 768), (768, 1152, 1536), (1536, 1920, WIDE))
OUT_PARTS = ((0, 384, 768), (768, 1152, 1408), (1408, 1792, HALF))


class Place:
    def __init__(self):
        self.grp, ep, self.core = lax.axis_index("grp"), lax.axis_index("ep"), lax.axis_index("tp")
        self.expert = self.grp * 32 + ep
        self.at = (ep // 8, self.grp * 2 + (ep // 4) % 2, ep % 4)
        self.sibling = self.device(self.at, 1 - self.core)

    def device(self, at, core):
        x, y, z = at
        return (y // 2, (x * 2 + y % 2) * 4 + z, core)

    def along(self, dim, step):
        return (self.at[dim] + step + 4) % 4

    def neighbour(self, dim, step):
        at = list(self.at)
        at[dim] = self.along(dim, step)
        return self.device(at, self.core)

    def block(self, p, step):
        index = list(self.at)
        index[ORDERS[p][0]] = self.along(ORDERS[p][0], step)
        return tuple(index)

    def row(self, p, second, third):
        a, b, d = ORDERS[p]
        index = [None] * 3
        index[a], index[b], index[d] = slice(None), self.along(b, second), self.along(d, third)
        return tuple(index)

    def slab(self, p, second):
        index = [slice(None)] * 3
        index[ORDERS[p][1]] = self.along(ORDERS[p][1], second)
        return tuple(index)

    def group(self, p, third):
        a, b, d = ORDERS[p]
        index = [None] * 3
        index[a], index[b], index[d] = slice(None), slice(None), self.along(d, third)
        return tuple(index)


def greet(place):
    friends = [place.neighbour(dim, step) for dim in range(3) for step in STEPS] + [place.sibling]
    barrier = pltpu.get_barrier_semaphore()
    for device in friends:
        pl.semaphore_signal(barrier, inc=1, device_id=device, device_id_type=MESH)
    return lambda: pl.semaphore_wait(barrier, len(friends))


def remote(src, dst, send, recv, device):
    return pltpu.make_async_remote_copy(
        src_ref=src, dst_ref=dst, send_sem=send, recv_sem=recv, device_id=device, device_id_type=MESH
    )


GATHER_SEMS = [
    pltpu.SemaphoreType.DMA((2, 3, 3)),
    pltpu.SemaphoreType.DMA((2, 3, 3)),
    pltpu.SemaphoreType.DMA((2, 3, 4, 2)),
    pltpu.SemaphoreType.DMA((2, 3, 4, 2)),
    pltpu.SemaphoreType.DMA((2, 3, 4)),
]
REDUCE_SEMS = [
    pltpu.SemaphoreType.DMA((2, 3, 4)),
    pltpu.SemaphoreType.DMA((2, 3, 4, 2, 3)),
    pltpu.SemaphoreType.DMA((2, 3, 3)),
    pltpu.SemaphoreType.DMA((2, 3, 3)),
]


class Gather:
    def __init__(self, place, buf, parts, sems):
        self.place, self.buf, self.parts = place, buf, parts
        self.block_sem, self.row_sem, self.near_sem, self.far_sem, self.across_sem = sems
        self.started = []

    def go(self, copy):
        copy.start()
        self.started.append(copy)

    def view(self, p, index, half=None, plane=None):
        low, mid, high = self.parts[p]
        if half is not None:
            low, high = ((low, mid), (mid, high))[half]
        plane = self.place.core if plane is None else plane
        return self.buf.at[(plane,) + index + (slice(None), pl.ds(low, high - low))]

    def copy(self, view, sem, spot, device):
        return remote(view, view, sem.at[(0,) + spot], sem.at[(1,) + spot], device)

    def block(self, p, i, step):
        view = self.view(p, self.place.block(p, step))
        return self.copy(view, self.block_sem, (p, i), self.place.neighbour(ORDERS[p][0], STEPS[i]))

    def row(self, p, i, step):
        view = self.view(p, self.place.row(p, step, 0))
        return self.copy(view, self.row_sem, (p, i), self.place.neighbour(ORDERS[p][1], STEPS[i]))

    def near(self, p, r, way, step):
        view = self.view(p, self.place.row(p, ROWS_OUT[r], step))
        return self.copy(view, self.near_sem, (p, r, way), self.place.neighbour(ORDERS[p][2], STEPS[way]))

    def far(self, p, r, way, step):
        view = self.view(p, self.place.row(p, ROWS_OUT[r], step), half=way)
        return self.copy(view, self.far_sem, (p, r, way), self.place.neighbour(ORDERS[p][2], STEPS[way]))

    def across(self, p, g, plane):
        view = self.view(p, self.place.group(p, ROWS_OUT[g]), plane=plane)
        return self.copy(view, self.across_sem, (p, g), self.place.sibling)

    def send_blocks(self):
        for i in range(3):
            for p in range(3):
                self.go(self.block(p, i, 0))

    def send_rows(self):
        for p in range(3):
            for i in range(3):
                self.block(p, i, -STEPS[i]).wait_recv()
            for i in range(3):
                self.go(self.row(p, i, 0))
        self.spread(0)

    def spread(self, r):
        for p in range(3):
            for way in range(2):
                self.go(self.near(p, r, way, 0))

    def take_row(self, r):
        i = {-1: 0, 1: 1, 2: 2}[ROWS_OUT[r]]
        for p in range(3):
            self.row(p, i, -STEPS[i]).wait_recv()
        self.spread(r)

    def pass_on(self, r):
        for p in range(3):
            for way in range(2):
                self.near(p, r, way, -STEPS[way]).wait_recv()
                self.go(self.far(p, r, way, -STEPS[way]))

    def take_far(self, r):
        for p in range(3):
            for way in range(2):
                self.far(p, r, way, 2).wait_recv()

    def cross(self, g):
        for p in range(3):
            self.go(self.across(p, g, self.place.core))

    def take_across(self, p, g):
        self.across(p, g, 1 - self.place.core).wait_recv()

    def finish(self):
        for copy in self.started:
            copy.wait_send()


class Reduce:
    def __init__(self, place, total, pair_buf, boxes, row_boxes, block_boxes, sems):
        self.place, self.total, self.pair_buf = place, total, pair_buf
        self.boxes, self.row_boxes, self.block_boxes = boxes, row_boxes, block_boxes
        self.pair_sem, self.ring_sem, self.row_sem, self.block_sem = sems
        self.started = []

    def go(self, copy):
        copy.start()
        self.started.append(copy)

    def halves(self, p):
        low, mid, high = OUT_PARTS[p]
        return ((low, mid - low), (mid, high - mid))

    def pair(self, p, r):
        low, _, high = OUT_PARTS[p]
        spot = self.place.slab(p, ROWS_IN[r]) + (slice(None), pl.ds(low, high - low))
        return remote(
            self.total.at[(1 - self.place.core,) + spot], self.pair_buf.at[spot],
            self.pair_sem.at[0, p, r], self.pair_sem.at[1, p, r], self.place.sibling,
        )

    def ring(self, p, r, way, item, step, half):
        low, width = self.halves(p)[half]
        view = self.total.at[
            (self.place.core,) + self.place.row(p, ROWS_IN[r], step) + (slice(None), pl.ds(low, width))
        ]
        return remote(
            view, self.boxes[p].at[way, item, r, :, :, pl.ds(0, width)],
            self.ring_sem.at[0, p, r, way, item], self.ring_sem.at[1, p, r, way, item],
            self.place.neighbour(ORDERS[p][2], STEPS[way]),
        )

    def row(self, p, i, step):
        low, _, high = OUT_PARTS[p]
        view = self.total.at[(self.place.core,) + self.place.row(p, step, 0) + (slice(None), pl.ds(low, high - low))]
        return remote(
            view, self.row_boxes.at[i, :, :, pl.ds(low, high - low)],
            self.row_sem.at[0, p, i], self.row_sem.at[1, p, i], self.place.neighbour(ORDERS[p][1], STEPS[i]),
        )

    def block(self, p, i, step):
        low, _, high = OUT_PARTS[p]
        view = self.total.at[(self.place.core,) + self.place.block(p, step) + (slice(None), pl.ds(low, high - low))]
        return remote(
            view, self.block_boxes.at[i, :, pl.ds(low, high - low)],
            self.block_sem.at[0, p, i], self.block_sem.at[1, p, i], self.place.neighbour(ORDERS[p][0], STEPS[i]),
        )

    def add(self, p, row, low, width, sources):
        a = ORDERS[p][0]
        cols = pl.ds(low, width)

        @pl.loop(0, 4)
        def _(n):
            index = list(row)
            index[a] = n
            here = (self.place.core,) + tuple(index) + (slice(None), cols)
            value = self.total[here].astype(jnp.float32)
            for source in sources:
                value = value + source[n].astype(jnp.float32)
            self.total[here] = value.astype(jnp.bfloat16)

    def start_row(self, p, r):
        for way in range(2):
            self.go(self.ring(p, r, way, 0, 2, way))
        for way in range(2):
            self.go(self.ring(p, r, way, 1, STEPS[way], 1 - way))

    def pass_on(self, r):
        for p in range(3):
            for way in range(2):
                low, width = self.halves(p)[way]
                self.ring(p, r, way, 0, 0, way).wait_recv()
                self.add(
                    p, self.place.row(p, ROWS_IN[r], STEPS[way]), low, width,
                    [self.boxes[p].at[way, 0, r, :, :, pl.ds(0, width)]],
                )
                self.go(self.ring(p, r, way, 2, STEPS[way], way))

    def combine(self, r):
        for p in range(3):
            for half in range(2):
                low, width = self.halves(p)[half]
                self.ring(p, r, half, 2, 0, half).wait_recv()
                self.ring(p, r, 1 - half, 1, 0, half).wait_recv()
                self.add(
                    p, self.place.row(p, ROWS_IN[r], 0), low, width,
                    [
                        self.boxes[p].at[half, 2, r, :, :, pl.ds(0, width)],
                        self.boxes[p].at[1 - half, 1, r, :, :, pl.ds(0, width)],
                    ],
                )
            if ROWS_IN[r]:
                self.go(self.row(p, STEPS.index(ROWS_IN[r]), ROWS_IN[r]))

    def last_row(self):
        for p in range(3):
            low, _, high = OUT_PARTS[p]
            for i in range(3):
                self.row(p, i, 0).wait_recv()
            self.add(
                p, self.place.row(p, 0, 0), low, high - low,
                [self.row_boxes.at[i, :, :, pl.ds(low, high - low)] for i in range(3)],
            )
            for i in range(3):
                self.go(self.block(p, i, STEPS[i]))

    def last_block(self, buf):
        for p in range(3):
            low, _, high = OUT_PARTS[p]
            cols = pl.ds(low, high - low)
            for i in range(3):
                self.block(p, i, 0).wait_recv()
            here = (self.place.core,) + self.place.at + (slice(None), cols)
            value = self.total[here].astype(jnp.float32)
            for i in range(3):
                value = value + self.block_boxes[i, :, cols].astype(jnp.float32)
            buf[here] = (value * (1.0 / math.sqrt(TOKENS))).astype(jnp.bfloat16)

    def finish(self):
        for copy in self.started:
            copy.wait_send()


def gain_rows(gain_ref, number):
    return jnp.broadcast_to(gain_ref[pl.ds(number, 1), :], (128, 128)).T


def step_kernel(
    tokens_ref, ids_ref, weights_ref, tgain_ref, sgain_ref, eg, eu, ed, sg, su, sd, gate_out, up_out, down_out,
    x_buf, g_buf, total, pair_buf, w_teacher, down, acc_teacher, acc_gate, acc_up, grad_hidden,
    hid, hidden_t, pre_t, rows, other, box0, box1, box2, row_boxes, block_boxes, load_sem, first_sem, *sems
):
    place = Place()
    core = place.core
    greeted = greet(place)
    loads = []
    for q in range(4):
        cut = pl.ds(q * 1024, 1024)
        loads.append(
            [
                pltpu.make_async_copy(eg.at[cut], w_teacher.at[cut, pl.ds(0, FE)], load_sem.at[q, 0]),
                pltpu.make_async_copy(eu.at[cut], w_teacher.at[cut, pl.ds(FE, FE)], load_sem.at[q, 1]),
                pltpu.make_async_copy(sg.at[:, cut], gate_out.at[:, cut], load_sem.at[q, 2]),
                pltpu.make_async_copy(su.at[:, cut], up_out.at[:, cut], load_sem.at[q, 3]),
            ]
        )
    own_rows = pl.ds(pl.multiple_of(place.grp * OWN, 16), OWN)
    loads.append(
        [
            pltpu.make_async_copy(ed, down.at[pl.ds(0, FE)], load_sem.at[4, 0]),
            pltpu.make_async_copy(sd.at[own_rows], down.at[pl.ds(FE, OWN)], load_sem.at[4, 1]),
            pltpu.make_async_copy(sd, down_out, load_sem.at[4, 2]),
        ]
    )
    for bundle in loads:
        for load in bundle:
            load.start()

    wide = tokens_ref[...].astype(jnp.float32)
    scale_own = lax.rsqrt(jnp.mean(wide * wide, axis=-1, keepdims=True) + EPSILON)
    lane = lax.broadcasted_iota(jnp.int32, (8, META), 1)
    meta = jnp.where(lane >= 64, scale_own, 0.0)
    for k in range(8):
        meta = meta + jnp.where(lane == ids_ref[:, k:k + 1], weights_ref[:, k:k + 1], 0.0)
    meta_high = meta.astype(jnp.bfloat16).astype(jnp.float32)
    for h in range(2):
        rows[h, :, :HALF] = wide[:, h * HALF:(h + 1) * HALF]
    rows[0, :, HALF:] = meta_high
    rows[1, :, HALF:] = meta - meta_high
    down[FE + OWN:, :] = jnp.zeros((512 - FE - OWN, D), jnp.bfloat16)

    @pl.loop(0, 4)
    def _(x):
        for acc in (acc_teacher, acc_gate, acc_up, grad_hidden):
            acc[x] = jnp.zeros(acc.shape[1:], jnp.float32)

    greeted()
    first = remote(rows.at[1 - core], other, first_sem.at[0], first_sem.at[1], place.sibling)
    first.start()
    first.wait()
    mine, theirs = rows[core], other[...]
    top = jnp.where(core == 0, mine, theirs)
    bottom = jnp.where(core == 0, theirs, mine)
    x_buf[(core,) + place.at] = jnp.concatenate([top, bottom], axis=0).astype(jnp.bfloat16)

    def scale(q):
        for load in loads[q]:
            load.wait()

        @pl.loop(q * 8, q * 8 + 8)
        def _(n):
            cut = pl.ds(pl.multiple_of(n * 128, 128), 128)
            gain = gain_rows(tgain_ref, n)
            for t in range(2 * FE // 128):
                cols = pl.ds(t * 128, 128)
                w_teacher[cut, cols] = (w_teacher[cut, cols].astype(jnp.float32) * gain).astype(jnp.bfloat16)
            gain = sgain_ref[pl.ds(n, 1), :]
            for w in (gate_out, up_out):
                w[:, cut] = (w[:, cut].astype(jnp.float32) * gain).astype(jnp.bfloat16)

    def forward(p, g, plane):
        index = place.group(p, ROWS_OUT[g])
        low, _, high = IN_PARTS[p]
        width = min(high, HALF) - low
        lhs = x_buf[(plane,) + index + (slice(None), pl.ds(low, width))].reshape(256, width)
        depth = pl.ds(pl.multiple_of(plane * HALF + low, 128), width)

        def put(acc, cols, value):
            here = index + (slice(None), cols)
            acc[here] = acc[here] + value.reshape(4, 4, 16, value.shape[-1])

        put(acc_teacher, slice(None), jnp.dot(lhs, w_teacher[depth, :], preferred_element_type=jnp.float32))

        for acc, w in ((acc_gate, gate_out), (acc_up, up_out)):
            put(
                acc, slice(None),
                lax.dot_general(lhs, w[:, depth], (((1,), (1,)), ((), ())), preferred_element_type=jnp.float32),
            )

    ins = Gather(place, x_buf, IN_PARTS, sems[:5])

    def own(g):
        for p in range(3):
            forward(p, g, core)

    def theirs_too(g):
        for p in range(3):
            ins.take_across(p, g)
            forward(p, g, 1 - core)

    ins.send_blocks()
    scale(0)
    ins.send_rows()
    scale(1)
    ins.take_row(1)
    ins.take_row(2)
    scale(2)
    ins.pass_on(0)
    ins.take_row(3)
    ins.cross(0)
    scale(3)
    own(0)
    ins.pass_on(1)
    theirs_too(0)
    ins.pass_on(2)
    ins.pass_on(3)
    ins.cross(1)
    ins.cross(2)
    own(1)
    own(2)
    ins.take_far(0)
    ins.take_far(1)
    theirs_too(1)
    ins.take_far(2)
    ins.take_far(3)
    ins.cross(3)
    theirs_too(2)
    own(3)
    theirs_too(3)
    for load in loads[4]:
        load.wait()

    lanes = lax.broadcasted_iota(jnp.int32, (256, META), 1)

    def facts(x):
        known = sum(x_buf[h, x, :, :, :, pl.ds(HALF, META)].astype(jnp.float32) for h in range(2)).reshape(256, META)
        row_scale = jnp.sum(jnp.where(lanes == 64, known, 0.0), axis=1, keepdims=True)
        weight = jnp.sum(jnp.where(lanes == place.expert, known, 0.0), axis=1, keepdims=True)
        return row_scale, weight

    @pl.loop(0, 4)
    def _(x):
        row_scale, weight = facts(x)
        gate = acc_teacher[x, :, :, :, pl.ds(0, FE)].reshape(256, FE) * row_scale
        up = acc_teacher[x, :, :, :, pl.ds(FE, FE)].reshape(256, FE) * row_scale
        value = gate * jax.nn.sigmoid(gate) * up * -weight
        hid[x, :, :, :, pl.ds(0, FE)] = value.astype(jnp.bfloat16).reshape(4, 4, 16, FE)
        gate = acc_gate[x].reshape(256, FU) * row_scale
        up = acc_up[x].reshape(256, FU) * row_scale
        acc_gate[x] = gate.reshape(4, 4, 16, FU)
        acc_up[x] = up.reshape(4, 4, 16, FU)
        value = gate * jax.nn.sigmoid(gate) * up
        hidden_t[:, pl.ds(pl.multiple_of(x * 256, 256), 256)] = value.T.astype(jnp.bfloat16)
        half = jnp.where(place.grp == 0, value[:, :OWN], value[:, OWN:])
        half = jnp.concatenate([half, jnp.zeros((256, 128 - OWN), jnp.float32)], axis=1)
        hid[x, :, :, :, pl.ds(FE, 128)] = half.astype(jnp.bfloat16).reshape(4, 4, 16, 128)

    red = Reduce(place, total, pair_buf, (box0, box1, box2), row_boxes, block_boxes, sems[5:9])

    def multiply(p, r, plane, added):
        low, _, high = OUT_PARTS[p]
        width = high - low
        slab = place.slab(p, ROWS_IN[r])
        spot = slab + (slice(None), pl.ds(low, width))
        weights = pl.ds(pl.multiple_of(plane * HALF + low, 128), width)
        value = jnp.dot(
            hid[slab + (slice(None), slice(None))].reshape(256, 512), down[:, weights],
            preferred_element_type=jnp.float32,
        ).reshape(4, 4, 16, width)
        if added:
            value = value + pair_buf[spot].astype(jnp.float32)
        total[(plane,) + spot] = value.astype(jnp.bfloat16)

    for r in range(4):
        for p in range(3):
            multiply(p, r, 1 - core, False)
            red.go(red.pair(p, r))
    for r in range(4):
        for p in range(3):
            red.pair(p, r).wait_recv()
            multiply(p, r, core, True)
            red.start_row(p, r)
    red.pass_on(0)
    red.pass_on(1)
    red.combine(0)
    red.pass_on(2)
    red.combine(1)
    red.pass_on(3)
    red.combine(2)
    red.combine(3)
    red.last_row()
    red.last_block(g_buf)

    def backward(p, g):
        index = place.group(p, ROWS_OUT[g])
        low, _, high = OUT_PARTS[p]
        width = high - low
        value = sum(
            lax.dot_general(
                g_buf[(h,) + index + (slice(None), pl.ds(low, width))].reshape(256, width),
                down_out[:, pl.ds(h * HALF + low, width)], (((1,), (1,)), ((), ())),
                preferred_element_type=jnp.float32,
            )
            for h in range(2)
        ).reshape(4, 4, 16, FU)
        grad_hidden[index] = grad_hidden[index] + value

    outs = Gather(place, g_buf, OUT_PARTS, sems[9:14])

    def back(g):
        for p in range(3):
            outs.take_across(p, g)
            backward(p, g)

    outs.send_blocks()
    outs.send_rows()
    outs.take_row(1)
    outs.take_row(2)
    outs.pass_on(0)
    outs.take_row(3)
    outs.cross(0)
    outs.pass_on(1)
    back(0)
    outs.pass_on(2)
    outs.pass_on(3)
    outs.cross(1)
    outs.cross(2)
    outs.take_far(0)
    outs.take_far(1)
    back(1)
    outs.take_far(2)
    outs.take_far(3)
    outs.cross(3)
    back(2)
    back(3)

    @pl.loop(0, 4)
    def _(x):
        row_scale, _ = facts(x)
        gate, up = acc_gate[x].reshape(256, FU), acc_up[x].reshape(256, FU)
        sigma = jax.nn.sigmoid(gate)
        grad = grad_hidden[x].reshape(256, FU) * row_scale
        gate_part = grad * up * sigma * (1.0 + gate * (1.0 - sigma))
        up_part = grad * gate * sigma
        cols = pl.ds(pl.multiple_of(x * 256, 256), 256)
        pre_t[pl.ds(0, FU), cols] = gate_part.T.astype(jnp.bfloat16)
        pre_t[pl.ds(FU, FU), cols] = up_part.T.astype(jnp.bfloat16)

    for h in range(2):
        for t in range(HALF // 512):
            cols = pl.ds(t * 512, 512)
            spot = pl.ds(h * HALF + t * 512, 512)
            value = jnp.dot(
                pre_t[...], x_buf[h, :, :, :, :, cols].reshape(TOKENS, 512), preferred_element_type=jnp.float32
            )
            first_gain = h * 16 + t * 4
            gain = jnp.concatenate([sgain_ref[first_gain + i:first_gain + i + 1, :] for i in range(4)], axis=1)
            gate_out[:, spot] = (value[:FU] * gain).astype(jnp.bfloat16)
            up_out[:, spot] = (value[FU:] * gain).astype(jnp.bfloat16)
            value = jnp.dot(
                hidden_t[...], g_buf[h, :, :, :, :, cols].reshape(TOKENS, 512), preferred_element_type=jnp.float32
            )
            down_out[:, spot] = value.astype(jnp.bfloat16)

    ins.finish()
    red.finish()
    outs.finish()


def step(tokens, ids, weights, tgain, sgain, eg, eu, ed, sg, su, sd):
    bf16, f32 = jnp.bfloat16, jnp.float32
    vmem, hbm = pl.BlockSpec(memory_space=pltpu.VMEM), pl.BlockSpec(memory_space=pl.ANY)
    return pl.pallas_call(
        step_kernel,
        out_shape=(pltpu.VMEM((FU, D), bf16),) * 3,
        in_specs=[vmem] * 5 + [hbm] * 6,
        out_specs=[vmem] * 3,
        scratch_shapes=[
            pltpu.VMEM((2, 4, 4, 4, 16, WIDE), bf16),
            pltpu.VMEM((2, 4, 4, 4, 16, HALF), bf16),
            pltpu.VMEM((2, 4, 4, 4, 16, HALF), bf16),
            pltpu.VMEM((4, 4, 4, 16, HALF), bf16),
            pltpu.VMEM((D, 2 * FE), bf16),
            pltpu.VMEM((512, D), bf16),
            pltpu.VMEM((4, 4, 4, 16, 2 * FE), f32),
            pltpu.VMEM((4, 4, 4, 16, FU), f32),
            pltpu.VMEM((4, 4, 4, 16, FU), f32),
            pltpu.VMEM((4, 4, 4, 16, FU), f32),
            pltpu.VMEM((4, 4, 4, 16, 512), bf16),
            pltpu.VMEM((FU, TOKENS), bf16),
            pltpu.VMEM((2 * FU, TOKENS), bf16),
            pltpu.VMEM((2, 8, WIDE), f32),
            pltpu.VMEM((8, WIDE), f32),
        ]
        + [pltpu.VMEM((2, 3, 4, 4, 16, 384), bf16)] * 3
        + [
            pltpu.VMEM((3, 4, 16, HALF), bf16),
            pltpu.VMEM((3, 16, HALF), bf16),
            pltpu.SemaphoreType.DMA((5, 4)),
            pltpu.SemaphoreType.DMA((2,)),
        ]
        + GATHER_SEMS
        + REDUCE_SEMS
        + GATHER_SEMS,
        compiler_params=pltpu.CompilerParams(collective_id=0, has_side_effects=True, vmem_limit_bytes=57 << 20),
        name="distill",
    )(tokens, ids, weights, tgain, sgain, eg, eu, ed, sg, su, sd)


def body(
    tokens, teacher_gain, student_gain, expert_ids, route_weights,
    expert_gate, expert_up, expert_down, student_gate, student_up, student_down,
):
    gate, up, down = step(
        tokens, expert_ids, route_weights, teacher_gain.reshape(32, 128), student_gain.reshape(32, 128),
        expert_gate[0], expert_up[0], expert_down[0], student_gate.T, student_up.T, student_down,
    )
    return gate.T, up.T, down


def solution(mesh):
    everywhere = ("grp", "ep", "tp")
    in_specs = (
        P(everywhere, None),
        P(),
        P(),
        P(everywhere, None),
        P(everywhere, None),
        P(("grp", "ep"), None, "tp"),
        P(("grp", "ep"), None, "tp"),
        P(("grp", "ep"), "tp", None),
        P(None, ("ep", "tp")),
        P(None, ("ep", "tp")),
        P(("ep", "tp"), None),
    )
    out_specs = (P(None, ("ep", "tp")), P(None, ("ep", "tp")), P(("ep", "tp"), None))
    return jax.shard_map(body, mesh=mesh, in_specs=in_specs, out_specs=out_specs, check_vma=False)
```

```python
import math

import jax
import jax.numpy as jnp
from jax import lax
from jax.experimental import pallas as pl
from jax.experimental.pallas import tpu as pltpu
from jax.sharding import PartitionSpec as P

EPSILON = 1e-06
D = 4096
HALF = 2048
META = 128
WIDE = HALF + META
TOKENS = 1024
FE = 384
FU = 224
OWN = 112
MESH = pl.DeviceIdType.MESH
ORDERS = ((0, 1, 2), (1, 2, 0), (2, 0, 1))
ROWS_OUT = (0, -1, 1, 2)
ROWS_IN = (2, 1, -1, 0)
STEPS = (1, -1, 2)
IN_PARTS = ((0, 384, 768), (768, 1152, 1536), (1536, 1920, WIDE))
OUT_PARTS = ((0, 384, 768), (768, 1152, 1408), (1408, 1792, HALF))


class Place:
    def __init__(self):
        self.grp, ep, self.core = lax.axis_index("grp"), lax.axis_index("ep"), lax.axis_index("tp")
        self.expert = self.grp * 32 + ep
        self.at = (ep // 8, self.grp * 2 + (ep // 4) % 2, ep % 4)
        self.sibling = self.device(self.at, 1 - self.core)

    def device(self, at, core):
        x, y, z = at
        return (y // 2, (x * 2 + y % 2) * 4 + z, core)

    def along(self, dim, step):
        return (self.at[dim] + step + 4) % 4

    def neighbour(self, dim, step):
        at = list(self.at)
        at[dim] = self.along(dim, step)
        return self.device(at, self.core)

    def block(self, p, step):
        index = list(self.at)
        index[ORDERS[p][0]] = self.along(ORDERS[p][0], step)
        return tuple(index)

    def row(self, p, second, third):
        a, b, d = ORDERS[p]
        index = [None] * 3
        index[a], index[b], index[d] = slice(None), self.along(b, second), self.along(d, third)
        return tuple(index)

    def slab(self, p, second):
        index = [slice(None)] * 3
        index[ORDERS[p][1]] = self.along(ORDERS[p][1], second)
        return tuple(index)

    def group(self, p, third):
        a, b, d = ORDERS[p]
        index = [None] * 3
        index[a], index[b], index[d] = slice(None), slice(None), self.along(d, third)
        return tuple(index)


def greet(place):
    friends = [place.neighbour(dim, step) for dim in range(3) for step in STEPS] + [place.sibling]
    barrier = pltpu.get_barrier_semaphore()
    for device in friends:
        pl.semaphore_signal(barrier, inc=1, device_id=device, device_id_type=MESH)
    return lambda: pl.semaphore_wait(barrier, len(friends))


def remote(src, dst, send, recv, device):
    return pltpu.make_async_remote_copy(
        src_ref=src, dst_ref=dst, send_sem=send, recv_sem=recv, device_id=device, device_id_type=MESH
    )


GATHER_SEMS = [
    pltpu.SemaphoreType.DMA((2, 3, 3)),
    pltpu.SemaphoreType.DMA((2, 3, 3)),
    pltpu.SemaphoreType.DMA((2, 3, 4, 2)),
    pltpu.SemaphoreType.DMA((2, 3, 4, 2)),
    pltpu.SemaphoreType.DMA((2, 3, 4)),
]
REDUCE_SEMS = [
    pltpu.SemaphoreType.DMA((2, 3, 4)),
    pltpu.SemaphoreType.DMA((2, 3, 4, 2, 3)),
    pltpu.SemaphoreType.DMA((2, 3, 3)),
    pltpu.SemaphoreType.DMA((2, 3, 3)),
]


class Gather:
    def __init__(self, place, buf, parts, sems):
        self.place, self.buf, self.parts = place, buf, parts
        self.block_sem, self.row_sem, self.near_sem, self.far_sem, self.across_sem = sems
        self.started = []

    def go(self, copy):
        copy.start()
        self.started.append(copy)

    def view(self, p, index, half=None, plane=None):
        low, mid, high = self.parts[p]
        if half is not None:
            low, high = ((low, mid), (mid, high))[half]
        plane = self.place.core if plane is None else plane
        return self.buf.at[(plane,) + index + (slice(None), pl.ds(low, high - low))]

    def copy(self, view, sem, spot, device):
        return remote(view, view, sem.at[(0,) + spot], sem.at[(1,) + spot], device)

    def block(self, p, i, step):
        view = self.view(p, self.place.block(p, step))
        return self.copy(view, self.block_sem, (p, i), self.place.neighbour(ORDERS[p][0], STEPS[i]))

    def row(self, p, i, step):
        view = self.view(p, self.place.row(p, step, 0))
        return self.copy(view, self.row_sem, (p, i), self.place.neighbour(ORDERS[p][1], STEPS[i]))

    def near(self, p, r, way, step):
        view = self.view(p, self.place.row(p, ROWS_OUT[r], step))
        return self.copy(view, self.near_sem, (p, r, way), self.place.neighbour(ORDERS[p][2], STEPS[way]))

    def far(self, p, r, way, step):
        view = self.view(p, self.place.row(p, ROWS_OUT[r], step), half=way)
        return self.copy(view, self.far_sem, (p, r, way), self.place.neighbour(ORDERS[p][2], STEPS[way]))

    def across(self, p, g, plane):
        view = self.view(p, self.place.group(p, ROWS_OUT[g]), plane=plane)
        return self.copy(view, self.across_sem, (p, g), self.place.sibling)

    def send_blocks(self):
        for i in range(3):
            for p in range(3):
                self.go(self.block(p, i, 0))

    def send_rows(self):
        for p in range(3):
            for i in range(3):
                self.block(p, i, -STEPS[i]).wait_recv()
            for i in range(3):
                self.go(self.row(p, i, 0))
        self.spread(0)

    def spread(self, r):
        for p in range(3):
            for way in range(2):
                self.go(self.near(p, r, way, 0))

    def take_row(self, r):
        i = {-1: 0, 1: 1, 2: 2}[ROWS_OUT[r]]
        for p in range(3):
            self.row(p, i, -STEPS[i]).wait_recv()
        self.spread(r)

    def pass_on(self, r):
        for p in range(3):
            for way in range(2):
                self.near(p, r, way, -STEPS[way]).wait_recv()
                self.go(self.far(p, r, way, -STEPS[way]))

    def take_far(self, r):
        for p in range(3):
            for way in range(2):
                self.far(p, r, way, 2).wait_recv()

    def cross(self, g):
        for p in range(3):
            self.go(self.across(p, g, self.place.core))

    def take_across(self, p, g):
        self.across(p, g, 1 - self.place.core).wait_recv()

    def finish(self):
        for copy in self.started:
            copy.wait_send()


class Reduce:
    def __init__(self, place, total, pair_buf, boxes, row_boxes, block_boxes, sems):
        self.place, self.total, self.pair_buf = place, total, pair_buf
        self.boxes, self.row_boxes, self.block_boxes = boxes, row_boxes, block_boxes
        self.pair_sem, self.ring_sem, self.row_sem, self.block_sem = sems
        self.started = []

    def go(self, copy):
        copy.start()
        self.started.append(copy)

    def halves(self, p):
        low, mid, high = OUT_PARTS[p]
        return ((low, mid - low), (mid, high - mid))

    def pair(self, p, r):
        low, _, high = OUT_PARTS[p]
        spot = self.place.slab(p, ROWS_IN[r]) + (slice(None), pl.ds(low, high - low))
        return remote(
            self.total.at[(1 - self.place.core,) + spot], self.pair_buf.at[spot],
            self.pair_sem.at[0, p, r], self.pair_sem.at[1, p, r], self.place.sibling,
        )

    def ring(self, p, r, way, item, step, half):
        low, width = self.halves(p)[half]
        view = self.total.at[
            (self.place.core,) + self.place.row(p, ROWS_IN[r], step) + (slice(None), pl.ds(low, width))
        ]
        return remote(
            view, self.boxes[p].at[way, item, r, :, :, pl.ds(0, width)],
            self.ring_sem.at[0, p, r, way, item], self.ring_sem.at[1, p, r, way, item],
            self.place.neighbour(ORDERS[p][2], STEPS[way]),
        )

    def row(self, p, i, step):
        low, _, high = OUT_PARTS[p]
        view = self.total.at[(self.place.core,) + self.place.row(p, step, 0) + (slice(None), pl.ds(low, high - low))]
        return remote(
            view, self.row_boxes.at[i, :, :, pl.ds(low, high - low)],
            self.row_sem.at[0, p, i], self.row_sem.at[1, p, i], self.place.neighbour(ORDERS[p][1], STEPS[i]),
        )

    def block(self, p, i, step):
        low, _, high = OUT_PARTS[p]
        view = self.total.at[(self.place.core,) + self.place.block(p, step) + (slice(None), pl.ds(low, high - low))]
        return remote(
            view, self.block_boxes.at[i, :, pl.ds(low, high - low)],
            self.block_sem.at[0, p, i], self.block_sem.at[1, p, i], self.place.neighbour(ORDERS[p][0], STEPS[i]),
        )

    def add(self, p, row, low, width, sources):
        a = ORDERS[p][0]
        cols = pl.ds(low, width)

        @pl.loop(0, 4)
        def _(n):
            index = list(row)
            index[a] = n
            here = (self.place.core,) + tuple(index) + (slice(None), cols)
            value = self.total[here].astype(jnp.float32)
            for source in sources:
                value = value + source[n].astype(jnp.float32)
            self.total[here] = value.astype(jnp.bfloat16)

    def start_row(self, p, r):
        for way in range(2):
            self.go(self.ring(p, r, way, 0, 2, way))
        for way in range(2):
            self.go(self.ring(p, r, way, 1, STEPS[way], 1 - way))

    def pass_on(self, r):
        for p in range(3):
            for way in range(2):
                low, width = self.halves(p)[way]
                self.ring(p, r, way, 0, 0, way).wait_recv()
                self.add(
                    p, self.place.row(p, ROWS_IN[r], STEPS[way]), low, width,
                    [self.boxes[p].at[way, 0, r, :, :, pl.ds(0, width)]],
                )
                self.go(self.ring(p, r, way, 2, STEPS[way], way))

    def combine(self, r):
        for p in range(3):
            for half in range(2):
                low, width = self.halves(p)[half]
                self.ring(p, r, half, 2, 0, half).wait_recv()
                self.ring(p, r, 1 - half, 1, 0, half).wait_recv()
                self.add(
                    p, self.place.row(p, ROWS_IN[r], 0), low, width,
                    [
                        self.boxes[p].at[half, 2, r, :, :, pl.ds(0, width)],
                        self.boxes[p].at[1 - half, 1, r, :, :, pl.ds(0, width)],
                    ],
                )
            if ROWS_IN[r]:
                self.go(self.row(p, STEPS.index(ROWS_IN[r]), ROWS_IN[r]))

    def last_row(self):
        for p in range(3):
            low, _, high = OUT_PARTS[p]
            for i in range(3):
                self.row(p, i, 0).wait_recv()
            self.add(
                p, self.place.row(p, 0, 0), low, high - low,
                [self.row_boxes.at[i, :, :, pl.ds(low, high - low)] for i in range(3)],
            )
            for i in range(3):
                self.go(self.block(p, i, STEPS[i]))

    def last_block(self, buf):
        for p in range(3):
            low, _, high = OUT_PARTS[p]
            cols = pl.ds(low, high - low)
            for i in range(3):
                self.block(p, i, 0).wait_recv()
            here = (self.place.core,) + self.place.at + (slice(None), cols)
            value = self.total[here].astype(jnp.float32)
            for i in range(3):
                value = value + self.block_boxes[i, :, cols].astype(jnp.float32)
            buf[here] = (value * (1.0 / math.sqrt(TOKENS))).astype(jnp.bfloat16)

    def finish(self):
        for copy in self.started:
            copy.wait_send()


def gain_rows(gain_ref, number):
    return jnp.broadcast_to(gain_ref[pl.ds(number, 1), :], (128, 128)).T


def step_kernel(
    tokens_ref, ids_ref, weights_ref, tgain_ref, sgain_ref, eg, eu, ed, sg, su, sd, gate_out, up_out, down_out,
    x_buf, g_buf, total, pair_buf, w_teacher, down, acc_teacher, acc_gate, acc_up, grad_hidden,
    hid, hidden_t, pre_t, rows, other, box0, box1, box2, row_boxes, block_boxes, load_sem, first_sem, *sems
):
    place = Place()
    core = place.core
    greeted = greet(place)
    loads = []
    for q in range(4):
        cut = pl.ds(q * 1024, 1024)
        loads.append(
            [
                pltpu.make_async_copy(eg.at[cut], w_teacher.at[cut, pl.ds(0, FE)], load_sem.at[q, 0]),
                pltpu.make_async_copy(eu.at[cut], w_teacher.at[cut, pl.ds(FE, FE)], load_sem.at[q, 1]),
                pltpu.make_async_copy(sg.at[:, cut], gate_out.at[:, cut], load_sem.at[q, 2]),
                pltpu.make_async_copy(su.at[:, cut], up_out.at[:, cut], load_sem.at[q, 3]),
            ]
        )
    own_rows = pl.ds(pl.multiple_of(place.grp * OWN, 16), OWN)
    loads.append(
        [
            pltpu.make_async_copy(ed, down.at[pl.ds(0, FE)], load_sem.at[4, 0]),
            pltpu.make_async_copy(sd.at[own_rows], down.at[pl.ds(FE, OWN)], load_sem.at[4, 1]),
            pltpu.make_async_copy(sd, down_out, load_sem.at[4, 2]),
        ]
    )
    for bundle in loads:
        for load in bundle:
            load.start()

    wide = tokens_ref[...].astype(jnp.float32)
    scale_own = lax.rsqrt(jnp.mean(wide * wide, axis=-1, keepdims=True) + EPSILON)
    lane = lax.broadcasted_iota(jnp.int32, (8, META), 1)
    meta = jnp.where(lane >= 64, scale_own, 0.0)
    for k in range(8):
        meta = meta + jnp.where(lane == ids_ref[:, k:k + 1], weights_ref[:, k:k + 1], 0.0)
    meta_high = meta.astype(jnp.bfloat16).astype(jnp.float32)
    for h in range(2):
        rows[h, :, :HALF] = wide[:, h * HALF:(h + 1) * HALF]
    rows[0, :, HALF:] = meta_high
    rows[1, :, HALF:] = meta - meta_high
    down[FE + OWN:, :] = jnp.zeros((512 - FE - OWN, D), jnp.bfloat16)

    @pl.loop(0, 4)
    def _(x):
        for acc in (acc_teacher, acc_gate, acc_up, grad_hidden):
            acc[x] = jnp.zeros(acc.shape[1:], jnp.float32)

    greeted()
    first = remote(rows.at[1 - core], other, first_sem.at[0], first_sem.at[1], place.sibling)
    first.start()
    first.wait()
    mine, theirs = rows[core], other[...]
    top = jnp.where(core == 0, mine, theirs)
    bottom = jnp.where(core == 0, theirs, mine)
    x_buf[(core,) + place.at] = jnp.concatenate([top, bottom], axis=0).astype(jnp.bfloat16)

    def scale(q):
        for load in loads[q]:
            load.wait()

        @pl.loop(q * 8, q * 8 + 8)
        def _(n):
            cut = pl.ds(pl.multiple_of(n * 128, 128), 128)
            gain = gain_rows(tgain_ref, n)
            for t in range(2 * FE // 128):
                cols = pl.ds(t * 128, 128)
                w_teacher[cut, cols] = (w_teacher[cut, cols].astype(jnp.float32) * gain).astype(jnp.bfloat16)
            gain = sgain_ref[pl.ds(n, 1), :]
            for w in (gate_out, up_out):
                w[:, cut] = (w[:, cut].astype(jnp.float32) * gain).astype(jnp.bfloat16)

    def forward(p, g, plane):
        index = place.group(p, ROWS_OUT[g])
        low, _, high = IN_PARTS[p]
        width = min(high, HALF) - low
        lhs = x_buf[(plane,) + index + (slice(None), pl.ds(low, width))].reshape(256, width)
        depth = pl.ds(pl.multiple_of(plane * HALF + low, 128), width)

        def put(acc, cols, value):
            here = index + (slice(None), cols)
            acc[here] = acc[here] + value.reshape(4, 4, 16, value.shape[-1])

        put(acc_teacher, slice(None), jnp.dot(lhs, w_teacher[depth, :], preferred_element_type=jnp.float32))

        for acc, w in ((acc_gate, gate_out), (acc_up, up_out)):
            put(
                acc, slice(None),
                lax.dot_general(lhs, w[:, depth], (((1,), (1,)), ((), ())), preferred_element_type=jnp.float32),
            )

    ins = Gather(place, x_buf, IN_PARTS, sems[:5])

    def own(g):
        for p in range(3):
            forward(p, g, core)

    def theirs_too(g):
        for p in range(3):
            ins.take_across(p, g)
            forward(p, g, 1 - core)

    ins.send_blocks()
    scale(0)
    ins.send_rows()
    scale(1)
    ins.take_row(1)
    ins.take_row(2)
    scale(2)
    ins.pass_on(0)
    ins.take_row(3)
    ins.cross(0)
    scale(3)
    own(0)
    ins.pass_on(1)
    theirs_too(0)
    ins.pass_on(2)
    ins.pass_on(3)
    ins.cross(1)
    ins.cross(2)
    own(1)
    own(2)
    ins.take_far(0)
    ins.take_far(1)
    theirs_too(1)
    ins.take_far(2)
    ins.take_far(3)
    ins.cross(3)
    theirs_too(2)
    own(3)
    theirs_too(3)
    for load in loads[4]:
        load.wait()

    lanes = lax.broadcasted_iota(jnp.int32, (256, META), 1)

    def facts(x):
        known = sum(x_buf[h, x, :, :, :, pl.ds(HALF, META)].astype(jnp.float32) for h in range(2)).reshape(256, META)
        row_scale = jnp.sum(jnp.where(lanes == 64, known, 0.0), axis=1, keepdims=True)
        weight = jnp.sum(jnp.where(lanes == place.expert, known, 0.0), axis=1, keepdims=True)
        return row_scale, weight

    @pl.loop(0, 4)
    def _(x):
        row_scale, weight = facts(x)
        gate = acc_teacher[x, :, :, :, pl.ds(0, FE)].reshape(256, FE) * row_scale
        up = acc_teacher[x, :, :, :, pl.ds(FE, FE)].reshape(256, FE) * row_scale
        value = gate * jax.nn.sigmoid(gate) * up * -weight
        hid[x, :, :, :, pl.ds(0, FE)] = value.astype(jnp.bfloat16).reshape(4, 4, 16, FE)
        gate = acc_gate[x].reshape(256, FU) * row_scale
        up = acc_up[x].reshape(256, FU) * row_scale
        acc_gate[x] = gate.reshape(4, 4, 16, FU)
        acc_up[x] = up.reshape(4, 4, 16, FU)
        value = gate * jax.nn.sigmoid(gate) * up
        hidden_t[:, pl.ds(pl.multiple_of(x * 256, 256), 256)] = value.T.astype(jnp.bfloat16)
        half = jnp.where(place.grp == 0, value[:, :OWN], value[:, OWN:])
        half = jnp.concatenate([half, jnp.zeros((256, 128 - OWN), jnp.float32)], axis=1)
        hid[x, :, :, :, pl.ds(FE, 128)] = half.astype(jnp.bfloat16).reshape(4, 4, 16, 128)

    red = Reduce(place, total, pair_buf, (box0, box1, box2), row_boxes, block_boxes, sems[5:9])

    def multiply(p, r, plane, added):
        low, _, high = OUT_PARTS[p]
        width = high - low
        slab = place.slab(p, ROWS_IN[r])
        spot = slab + (slice(None), pl.ds(low, width))
        weights = pl.ds(pl.multiple_of(plane * HALF + low, 128), width)
        value = jnp.dot(
            hid[slab + (slice(None), slice(None))].reshape(256, 512), down[:, weights],
            preferred_element_type=jnp.float32,
        ).reshape(4, 4, 16, width)
        if added:
            value = value + pair_buf[spot].astype(jnp.float32)
        total[(plane,) + spot] = value.astype(jnp.bfloat16)

    for r in range(4):
        for p in range(3):
            multiply(p, r, 1 - core, False)
            red.go(red.pair(p, r))
    for r in range(4):
        for p in range(3):
            red.pair(p, r).wait_recv()
            multiply(p, r, core, True)
            red.start_row(p, r)
    red.pass_on(0)
    red.pass_on(1)
    red.combine(0)
    red.pass_on(2)
    red.combine(1)
    red.pass_on(3)
    red.combine(2)
    red.combine(3)
    red.last_row()
    red.last_block(g_buf)

    def backward(p, g):
        index = place.group(p, ROWS_OUT[g])
        low, _, high = OUT_PARTS[p]
        width = high - low
        value = sum(
            lax.dot_general(
                g_buf[(h,) + index + (slice(None), pl.ds(low, width))].reshape(256, width),
                down_out[:, pl.ds(h * HALF + low, width)], (((1,), (1,)), ((), ())),
                preferred_element_type=jnp.float32,
            )
            for h in range(2)
        ).reshape(4, 4, 16, FU)
        grad_hidden[index] = grad_hidden[index] + value

    outs = Gather(place, g_buf, OUT_PARTS, sems[9:14])

    def back(g):
        for p in range(3):
            outs.take_across(p, g)
            backward(p, g)

    outs.send_blocks()
    ins.finish()
    outs.send_rows()
    red.finish()
    outs.take_row(1)
    outs.take_row(2)
    outs.take_row(3)
    outs.cross(0)

    @pl.loop(0, 4)
    def _(x):
        row_scale, _ = facts(x)
        gate, up = acc_gate[x].reshape(256, FU), acc_up[x].reshape(256, FU)
        sigma = jax.nn.sigmoid(gate)
        acc_gate[x] = (row_scale * up * sigma * (1.0 + gate * (1.0 - sigma))).reshape(4, 4, 16, FU)
        acc_up[x] = (row_scale * gate * sigma).reshape(4, 4, 16, FU)

    outs.pass_on(0)
    outs.pass_on(1)
    back(0)
    outs.pass_on(2)
    outs.pass_on(3)
    outs.cross(1)
    outs.cross(2)
    outs.take_far(0)
    outs.take_far(1)
    back(1)
    outs.take_far(2)
    outs.take_far(3)
    outs.cross(3)
    back(2)
    outs.finish()
    back(3)

    @pl.loop(0, 4)
    def _(x):
        grad = grad_hidden[x].reshape(256, FU)
        cols = pl.ds(pl.multiple_of(x * 256, 256), 256)
        pre_t[pl.ds(0, FU), cols] = (grad * acc_gate[x].reshape(256, FU)).T.astype(jnp.bfloat16)
        pre_t[pl.ds(FU, FU), cols] = (grad * acc_up[x].reshape(256, FU)).T.astype(jnp.bfloat16)

    for h in range(2):
        for t in range(HALF // 512):
            cols = pl.ds(t * 512, 512)
            spot = pl.ds(h * HALF + t * 512, 512)
            value = jnp.dot(
                pre_t[...], x_buf[h, :, :, :, :, cols].reshape(TOKENS, 512), preferred_element_type=jnp.float32
            )
            first_gain = h * 16 + t * 4
            gain = jnp.concatenate([sgain_ref[first_gain + i:first_gain + i + 1, :] for i in range(4)], axis=1)
            gate_out[:, spot] = (value[:FU] * gain).astype(jnp.bfloat16)
            up_out[:, spot] = (value[FU:] * gain).astype(jnp.bfloat16)
            value = jnp.dot(
                hidden_t[...], g_buf[h, :, :, :, :, cols].reshape(TOKENS, 512), preferred_element_type=jnp.float32
            )
            down_out[:, spot] = value.astype(jnp.bfloat16)


def step(tokens, ids, weights, tgain, sgain, eg, eu, ed, sg, su, sd):
    bf16, f32 = jnp.bfloat16, jnp.float32
    vmem, hbm = pl.BlockSpec(memory_space=pltpu.VMEM), pl.BlockSpec(memory_space=pl.ANY)
    return pl.pallas_call(
        step_kernel,
        out_shape=(pltpu.VMEM((FU, D), bf16),) * 3,
        in_specs=[vmem] * 5 + [hbm] * 6,
        out_specs=[vmem] * 3,
        scratch_shapes=[
            pltpu.VMEM((2, 4, 4, 4, 16, WIDE), bf16),
            pltpu.VMEM((2, 4, 4, 4, 16, HALF), bf16),
            pltpu.VMEM((2, 4, 4, 4, 16, HALF), bf16),
            pltpu.VMEM((4, 4, 4, 16, HALF), bf16),
            pltpu.VMEM((D, 2 * FE), bf16),
            pltpu.VMEM((512, D), bf16),
            pltpu.VMEM((4, 4, 4, 16, 2 * FE), f32),
            pltpu.VMEM((4, 4, 4, 16, FU), f32),
            pltpu.VMEM((4, 4, 4, 16, FU), f32),
            pltpu.VMEM((4, 4, 4, 16, FU), f32),
            pltpu.VMEM((4, 4, 4, 16, 512), bf16),
            pltpu.VMEM((FU, TOKENS), bf16),
            pltpu.VMEM((2 * FU, TOKENS), bf16),
            pltpu.VMEM((2, 8, WIDE), f32),
            pltpu.VMEM((8, WIDE), f32),
        ]
        + [pltpu.VMEM((2, 3, 4, 4, 16, 384), bf16)] * 3
        + [
            pltpu.VMEM((3, 4, 16, HALF), bf16),
            pltpu.VMEM((3, 16, HALF), bf16),
            pltpu.SemaphoreType.DMA((5, 4)),
            pltpu.SemaphoreType.DMA((2,)),
        ]
        + GATHER_SEMS
        + REDUCE_SEMS
        + GATHER_SEMS,
        compiler_params=pltpu.CompilerParams(collective_id=0, has_side_effects=True, vmem_limit_bytes=57 << 20),
        name="distill",
    )(tokens, ids, weights, tgain, sgain, eg, eu, ed, sg, su, sd)


def body(
    tokens, teacher_gain, student_gain, expert_ids, route_weights,
    expert_gate, expert_up, expert_down, student_gate, student_up, student_down,
):
    gate, up, down = step(
        tokens, expert_ids, route_weights, teacher_gain.reshape(32, 128), student_gain.reshape(32, 128),
        expert_gate[0], expert_up[0], expert_down[0], student_gate.T, student_up.T, student_down,
    )
    return gate.T, up.T, down


def solution(mesh):
    everywhere = ("grp", "ep", "tp")
    in_specs = (
        P(everywhere, None),
        P(),
        P(),
        P(everywhere, None),
        P(everywhere, None),
        P(("grp", "ep"), None, "tp"),
        P(("grp", "ep"), None, "tp"),
        P(("grp", "ep"), "tp", None),
        P(None, ("ep", "tp")),
        P(None, ("ep", "tp")),
        P(("ep", "tp"), None),
    )
    out_specs = (P(None, ("ep", "tp")), P(None, ("ep", "tp")), P(("ep", "tp"), None))
    return jax.shard_map(body, mesh=mesh, in_specs=in_specs, out_specs=out_specs, check_vma=False)
```

```python
import math

import jax
import jax.numpy as jnp
from jax import lax
from jax.experimental import pallas as pl
from jax.experimental.pallas import tpu as pltpu
from jax.sharding import PartitionSpec as P

EPSILON = 1e-06
D = 4096
HALF = 2048
META = 128
WIDE = HALF + META
TOKENS = 1024
FE = 384
FU = 224
OWN = 112
MESH = pl.DeviceIdType.MESH
ORDERS = ((0, 1, 2), (1, 2, 0), (2, 0, 1))
ROWS_OUT = (0, -1, 1, 2)
ROWS_IN = (2, 1, -1, 0)
STEPS = (1, -1, 2)
IN_PARTS = ((0, 384, 768), (768, 1152, 1536), (1536, 1920, WIDE))
OUT_PARTS = ((0, 384, 768), (768, 1152, 1408), (1408, 1792, HALF))


class Place:
    def __init__(self):
        self.grp, ep, self.core = lax.axis_index("grp"), lax.axis_index("ep"), lax.axis_index("tp")
        self.expert = self.grp * 32 + ep
        self.at = (ep // 8, self.grp * 2 + (ep // 4) % 2, ep % 4)
        self.sibling = self.device(self.at, 1 - self.core)

    def device(self, at, core):
        x, y, z = at
        return (y // 2, (x * 2 + y % 2) * 4 + z, core)

    def along(self, dim, step):
        return (self.at[dim] + step + 4) % 4

    def neighbour(self, dim, step):
        at = list(self.at)
        at[dim] = self.along(dim, step)
        return self.device(at, self.core)

    def block(self, p, step):
        index = list(self.at)
        index[ORDERS[p][0]] = self.along(ORDERS[p][0], step)
        return tuple(index)

    def row(self, p, second, third):
        a, b, d = ORDERS[p]
        index = [None] * 3
        index[a], index[b], index[d] = slice(None), self.along(b, second), self.along(d, third)
        return tuple(index)

    def slab(self, p, second):
        index = [slice(None)] * 3
        index[ORDERS[p][1]] = self.along(ORDERS[p][1], second)
        return tuple(index)

    def group(self, p, third):
        a, b, d = ORDERS[p]
        index = [None] * 3
        index[a], index[b], index[d] = slice(None), slice(None), self.along(d, third)
        return tuple(index)


def greet(place):
    friends = [place.neighbour(dim, step) for dim in range(3) for step in STEPS] + [place.sibling]
    barrier = pltpu.get_barrier_semaphore()
    for device in friends:
        pl.semaphore_signal(barrier, inc=1, device_id=device, device_id_type=MESH)
    return lambda: pl.semaphore_wait(barrier, len(friends))


def remote(src, dst, send, recv, device):
    return pltpu.make_async_remote_copy(
        src_ref=src, dst_ref=dst, send_sem=send, recv_sem=recv, device_id=device, device_id_type=MESH
    )


GATHER_SEMS = [
    pltpu.SemaphoreType.DMA((2, 3, 3)),
    pltpu.SemaphoreType.DMA((2, 3, 3)),
    pltpu.SemaphoreType.DMA((2, 3, 4, 2)),
    pltpu.SemaphoreType.DMA((2, 3, 4, 2)),
    pltpu.SemaphoreType.DMA((2, 3, 4)),
]
REDUCE_SEMS = [
    pltpu.SemaphoreType.DMA((2, 3, 4)),
    pltpu.SemaphoreType.DMA((2, 3, 4, 2, 3)),
    pltpu.SemaphoreType.DMA((2, 3, 3)),
    pltpu.SemaphoreType.DMA((2, 3, 3)),
]


class Gather:
    def __init__(self, place, buf, parts, sems):
        self.place, self.buf, self.parts = place, buf, parts
        self.block_sem, self.row_sem, self.near_sem, self.far_sem, self.across_sem = sems
        self.started = []

    def go(self, copy):
        copy.start()
        self.started.append(copy)

    def view(self, p, index, half=None, plane=None):
        low, mid, high = self.parts[p]
        if half is not None:
            low, high = ((low, mid), (mid, high))[half]
        plane = self.place.core if plane is None else plane
        return self.buf.at[(plane,) + index + (slice(None), pl.ds(low, high - low))]

    def copy(self, view, sem, spot, device):
        return remote(view, view, sem.at[(0,) + spot], sem.at[(1,) + spot], device)

    def block(self, p, i, step):
        view = self.view(p, self.place.block(p, step))
        return self.copy(view, self.block_sem, (p, i), self.place.neighbour(ORDERS[p][0], STEPS[i]))

    def row(self, p, i, step):
        view = self.view(p, self.place.row(p, step, 0))
        return self.copy(view, self.row_sem, (p, i), self.place.neighbour(ORDERS[p][1], STEPS[i]))

    def near(self, p, r, way, step):
        view = self.view(p, self.place.row(p, ROWS_OUT[r], step))
        return self.copy(view, self.near_sem, (p, r, way), self.place.neighbour(ORDERS[p][2], STEPS[way]))

    def far(self, p, r, way, step):
        view = self.view(p, self.place.row(p, ROWS_OUT[r], step), half=way)
        return self.copy(view, self.far_sem, (p, r, way), self.place.neighbour(ORDERS[p][2], STEPS[way]))

    def across(self, p, g, plane):
        view = self.view(p, self.place.group(p, ROWS_OUT[g]), plane=plane)
        return self.copy(view, self.across_sem, (p, g), self.place.sibling)

    def send_blocks(self):
        for i in range(3):
            for p in range(3):
                self.go(self.block(p, i, 0))

    def send_rows(self):
        for p in range(3):
            for i in range(3):
                self.block(p, i, -STEPS[i]).wait_recv()
            for i in range(3):
                self.go(self.row(p, i, 0))
        self.spread(0)

    def spread(self, r):
        for p in range(3):
            for way in range(2):
                self.go(self.near(p, r, way, 0))

    def take_row(self, r):
        i = {-1: 0, 1: 1, 2: 2}[ROWS_OUT[r]]
        for p in range(3):
            self.row(p, i, -STEPS[i]).wait_recv()
        self.spread(r)

    def pass_on(self, r):
        for p in range(3):
            for way in range(2):
                self.near(p, r, way, -STEPS[way]).wait_recv()
                self.go(self.far(p, r, way, -STEPS[way]))

    def take_far(self, r):
        for p in range(3):
            for way in range(2):
                self.far(p, r, way, 2).wait_recv()

    def cross(self, g):
        for p in range(3):
            self.go(self.across(p, g, self.place.core))

    def take_across(self, p, g):
        self.across(p, g, 1 - self.place.core).wait_recv()

    def finish(self):
        for copy in self.started:
            copy.wait_send()


class Reduce:
    def __init__(self, place, total, pair_buf, boxes, row_boxes, block_boxes, sems):
        self.place, self.total, self.pair_buf = place, total, pair_buf
        self.boxes, self.row_boxes, self.block_boxes = boxes, row_boxes, block_boxes
        self.pair_sem, self.ring_sem, self.row_sem, self.block_sem = sems
        self.started = []

    def go(self, copy):
        copy.start()
        self.started.append(copy)

    def halves(self, p):
        low, mid, high = OUT_PARTS[p]
        return ((low, mid - low), (mid, high - mid))

    def pair(self, p, r):
        low, _, high = OUT_PARTS[p]
        spot = self.place.slab(p, ROWS_IN[r]) + (slice(None), pl.ds(low, high - low))
        return remote(
            self.total.at[(1 - self.place.core,) + spot], self.pair_buf.at[spot],
            self.pair_sem.at[0, p, r], self.pair_sem.at[1, p, r], self.place.sibling,
        )

    def ring(self, p, r, way, item, step, half):
        low, width = self.halves(p)[half]
        view = self.total.at[
            (self.place.core,) + self.place.row(p, ROWS_IN[r], step) + (slice(None), pl.ds(low, width))
        ]
        return remote(
            view, self.boxes[p].at[way, item, r, :, :, pl.ds(0, width)],
            self.ring_sem.at[0, p, r, way, item], self.ring_sem.at[1, p, r, way, item],
            self.place.neighbour(ORDERS[p][2], STEPS[way]),
        )

    def row(self, p, i, step):
        low, _, high = OUT_PARTS[p]
        view = self.total.at[(self.place.core,) + self.place.row(p, step, 0) + (slice(None), pl.ds(low, high - low))]
        return remote(
            view, self.row_boxes.at[i, :, :, pl.ds(low, high - low)],
            self.row_sem.at[0, p, i], self.row_sem.at[1, p, i], self.place.neighbour(ORDERS[p][1], STEPS[i]),
        )

    def block(self, p, i, step):
        low, _, high = OUT_PARTS[p]
        view = self.total.at[(self.place.core,) + self.place.block(p, step) + (slice(None), pl.ds(low, high - low))]
        return remote(
            view, self.block_boxes.at[i, :, pl.ds(low, high - low)],
            self.block_sem.at[0, p, i], self.block_sem.at[1, p, i], self.place.neighbour(ORDERS[p][0], STEPS[i]),
        )

    def add(self, p, row, low, width, sources):
        a = ORDERS[p][0]
        cols = pl.ds(low, width)

        @pl.loop(0, 4)
        def _(n):
            index = list(row)
            index[a] = n
            here = (self.place.core,) + tuple(index) + (slice(None), cols)
            value = self.total[here].astype(jnp.float32)
            for source in sources:
                value = value + source[n].astype(jnp.float32)
            self.total[here] = value.astype(jnp.bfloat16)

    def start_row(self, p, r):
        for way in range(2):
            self.go(self.ring(p, r, way, 0, 2, way))
        for way in range(2):
            self.go(self.ring(p, r, way, 1, STEPS[way], 1 - way))

    def pass_on(self, r):
        for p in range(3):
            for way in range(2):
                low, width = self.halves(p)[way]
                self.ring(p, r, way, 0, 0, way).wait_recv()
                self.add(
                    p, self.place.row(p, ROWS_IN[r], STEPS[way]), low, width,
                    [self.boxes[p].at[way, 0, r, :, :, pl.ds(0, width)]],
                )
                self.go(self.ring(p, r, way, 2, STEPS[way], way))

    def combine(self, r):
        for p in range(3):
            for half in range(2):
                low, width = self.halves(p)[half]
                self.ring(p, r, half, 2, 0, half).wait_recv()
                self.ring(p, r, 1 - half, 1, 0, half).wait_recv()
                self.add(
                    p, self.place.row(p, ROWS_IN[r], 0), low, width,
                    [
                        self.boxes[p].at[half, 2, r, :, :, pl.ds(0, width)],
                        self.boxes[p].at[1 - half, 1, r, :, :, pl.ds(0, width)],
                    ],
                )
            if ROWS_IN[r]:
                self.go(self.row(p, STEPS.index(ROWS_IN[r]), ROWS_IN[r]))

    def last_row(self):
        for p in range(3):
            low, _, high = OUT_PARTS[p]
            for i in range(3):
                self.row(p, i, 0).wait_recv()
            self.add(
                p, self.place.row(p, 0, 0), low, high - low,
                [self.row_boxes.at[i, :, :, pl.ds(low, high - low)] for i in range(3)],
            )
            for i in range(3):
                self.go(self.block(p, i, STEPS[i]))

    def last_block(self, buf):
        for p in range(3):
            low, _, high = OUT_PARTS[p]
            cols = pl.ds(low, high - low)
            for i in range(3):
                self.block(p, i, 0).wait_recv()
            here = (self.place.core,) + self.place.at + (slice(None), cols)
            value = self.total[here].astype(jnp.float32)
            for i in range(3):
                value = value + self.block_boxes[i, :, cols].astype(jnp.float32)
            buf[here] = (value * (1.0 / math.sqrt(TOKENS))).astype(jnp.bfloat16)

    def finish(self):
        for copy in self.started:
            copy.wait_send()


def gain_rows(gain_ref, number):
    return jnp.broadcast_to(gain_ref[pl.ds(number, 1), :], (128, 128)).T


def step_kernel(
    tokens_ref, ids_ref, weights_ref, tgain_ref, sgain_ref, eg, eu, ed, sg, su, sd, gate_out, up_out, down_out,
    x_buf, g_buf, total, pair_buf, w_teacher, down, acc_teacher, acc_gate, acc_up, grad_hidden,
    hid, hidden, down_sum, pre_t, rows, other, box0, box1, box2, row_boxes, block_boxes, load_sem, first_sem, *sems
):
    place = Place()
    core = place.core
    greeted = greet(place)
    loads = []
    for q in range(4):
        cut = pl.ds(q * 1024, 1024)
        loads.append(
            [
                pltpu.make_async_copy(eg.at[cut], w_teacher.at[cut, pl.ds(0, FE)], load_sem.at[q, 0]),
                pltpu.make_async_copy(eu.at[cut], w_teacher.at[cut, pl.ds(FE, FE)], load_sem.at[q, 1]),
                pltpu.make_async_copy(sg.at[:, cut], gate_out.at[:, cut], load_sem.at[q, 2]),
                pltpu.make_async_copy(su.at[:, cut], up_out.at[:, cut], load_sem.at[q, 3]),
            ]
        )
    own_rows = pl.ds(pl.multiple_of(place.grp * OWN, 16), OWN)
    loads.append(
        [
            pltpu.make_async_copy(ed, down.at[pl.ds(0, FE)], load_sem.at[4, 0]),
            pltpu.make_async_copy(sd.at[own_rows], down.at[pl.ds(FE, OWN)], load_sem.at[4, 1]),
            pltpu.make_async_copy(sd, down_out, load_sem.at[4, 2]),
        ]
    )
    for bundle in loads:
        for load in bundle:
            load.start()

    wide = tokens_ref[...].astype(jnp.float32)
    scale_own = lax.rsqrt(jnp.mean(wide * wide, axis=-1, keepdims=True) + EPSILON)
    lane = lax.broadcasted_iota(jnp.int32, (8, META), 1)
    meta = jnp.where(lane >= 64, scale_own, 0.0)
    for k in range(8):
        meta = meta + jnp.where(lane == ids_ref[:, k:k + 1], weights_ref[:, k:k + 1], 0.0)
    meta_high = meta.astype(jnp.bfloat16).astype(jnp.float32)
    for h in range(2):
        rows[h, :, :HALF] = wide[:, h * HALF:(h + 1) * HALF]
    rows[0, :, HALF:] = meta_high
    rows[1, :, HALF:] = meta - meta_high
    down[FE + OWN:, :] = jnp.zeros((512 - FE - OWN, D), jnp.bfloat16)

    @pl.loop(0, 4)
    def _(x):
        for acc in (acc_teacher, acc_gate, acc_up, grad_hidden):
            acc[x] = jnp.zeros(acc.shape[1:], jnp.float32)

    greeted()
    first = remote(rows.at[1 - core], other, first_sem.at[0], first_sem.at[1], place.sibling)
    first.start()
    first.wait()
    mine, theirs = rows[core], other[...]
    top = jnp.where(core == 0, mine, theirs)
    bottom = jnp.where(core == 0, theirs, mine)
    x_buf[(core,) + place.at] = jnp.concatenate([top, bottom], axis=0).astype(jnp.bfloat16)

    def scale(q):
        for load in loads[q]:
            load.wait()

        @pl.loop(q * 8, q * 8 + 8)
        def _(n):
            cut = pl.ds(pl.multiple_of(n * 128, 128), 128)
            gain = gain_rows(tgain_ref, n)
            for t in range(2 * FE // 128):
                cols = pl.ds(t * 128, 128)
                w_teacher[cut, cols] = (w_teacher[cut, cols].astype(jnp.float32) * gain).astype(jnp.bfloat16)
            gain = sgain_ref[pl.ds(n, 1), :]
            for w in (gate_out, up_out):
                w[:, cut] = (w[:, cut].astype(jnp.float32) * gain).astype(jnp.bfloat16)

    def forward(p, g, plane):
        index = place.group(p, ROWS_OUT[g])
        low, _, high = IN_PARTS[p]
        width = min(high, HALF) - low
        lhs = x_buf[(plane,) + index + (slice(None), pl.ds(low, width))].reshape(256, width)
        depth = pl.ds(pl.multiple_of(plane * HALF + low, 128), width)

        def put(acc, cols, value):
            here = index + (slice(None), cols)
            acc[here] = acc[here] + value.reshape(4, 4, 16, value.shape[-1])

        put(acc_teacher, slice(None), jnp.dot(lhs, w_teacher[depth, :], preferred_element_type=jnp.float32))

        for acc, w in ((acc_gate, gate_out), (acc_up, up_out)):
            put(
                acc, slice(None),
                lax.dot_general(lhs, w[:, depth], (((1,), (1,)), ((), ())), preferred_element_type=jnp.float32),
            )

    ins = Gather(place, x_buf, IN_PARTS, sems[:5])

    def own(g):
        for p in range(3):
            forward(p, g, core)

    def theirs_too(g):
        for p in range(3):
            ins.take_across(p, g)
            forward(p, g, 1 - core)

    ins.send_blocks()
    scale(0)
    ins.send_rows()
    scale(1)
    ins.take_row(1)
    ins.take_row(2)
    scale(2)
    ins.pass_on(0)
    ins.take_row(3)
    ins.cross(0)
    scale(3)
    own(0)
    ins.pass_on(1)
    theirs_too(0)
    ins.pass_on(2)
    ins.pass_on(3)
    ins.cross(1)
    ins.cross(2)
    own(1)
    own(2)
    ins.take_far(0)
    ins.take_far(1)
    theirs_too(1)
    ins.take_far(2)
    ins.take_far(3)
    ins.cross(3)
    theirs_too(2)
    own(3)
    theirs_too(3)
    for load in loads[4]:
        load.wait()

    lanes = lax.broadcasted_iota(jnp.int32, (256, META), 1)

    def facts(x):
        known = sum(x_buf[h, x, :, :, :, pl.ds(HALF, META)].astype(jnp.float32) for h in range(2)).reshape(256, META)
        row_scale = jnp.sum(jnp.where(lanes == 64, known, 0.0), axis=1, keepdims=True)
        weight = jnp.sum(jnp.where(lanes == place.expert, known, 0.0), axis=1, keepdims=True)
        return row_scale, weight

    @pl.loop(0, 4)
    def _(x):
        row_scale, weight = facts(x)
        gate = acc_teacher[x, :, :, :, pl.ds(0, FE)].reshape(256, FE) * row_scale
        up = acc_teacher[x, :, :, :, pl.ds(FE, FE)].reshape(256, FE) * row_scale
        value = gate * jax.nn.sigmoid(gate) * up * -weight
        hid[x, :, :, :, pl.ds(0, FE)] = value.astype(jnp.bfloat16).reshape(4, 4, 16, FE)
        gate = acc_gate[x].reshape(256, FU) * row_scale
        up = acc_up[x].reshape(256, FU) * row_scale
        acc_gate[x] = gate.reshape(4, 4, 16, FU)
        acc_up[x] = up.reshape(4, 4, 16, FU)
        value = gate * jax.nn.sigmoid(gate) * up
        hidden[x] = value.astype(jnp.bfloat16).reshape(4, 4, 16, FU)
        half = jnp.where(place.grp == 0, value[:, :OWN], value[:, OWN:])
        half = jnp.concatenate([half, jnp.zeros((256, 128 - OWN), jnp.float32)], axis=1)
        hid[x, :, :, :, pl.ds(FE, 128)] = half.astype(jnp.bfloat16).reshape(4, 4, 16, 128)

    red = Reduce(place, total, pair_buf, (box0, box1, box2), row_boxes, block_boxes, sems[5:9])

    def multiply(p, r, plane, added):
        low, _, high = OUT_PARTS[p]
        width = high - low
        slab = place.slab(p, ROWS_IN[r])
        spot = slab + (slice(None), pl.ds(low, width))
        weights = pl.ds(pl.multiple_of(plane * HALF + low, 128), width)
        value = jnp.dot(
            hid[slab + (slice(None), slice(None))].reshape(256, 512), down[:, weights],
            preferred_element_type=jnp.float32,
        ).reshape(4, 4, 16, width)
        if added:
            value = value + pair_buf[spot].astype(jnp.float32)
        total[(plane,) + spot] = value.astype(jnp.bfloat16)

    for r in range(4):
        for p in range(3):
            multiply(p, r, 1 - core, False)
            red.go(red.pair(p, r))
    for r in range(4):
        for p in range(3):
            red.pair(p, r).wait_recv()
            multiply(p, r, core, True)
            red.start_row(p, r)
    red.pass_on(0)
    red.pass_on(1)
    red.combine(0)
    red.pass_on(2)
    red.combine(1)
    red.pass_on(3)
    red.combine(2)
    red.combine(3)
    red.last_row()
    red.last_block(g_buf)

    def backward(p, g):
        index = place.group(p, ROWS_OUT[g])
        low, _, high = OUT_PARTS[p]
        width = high - low
        value = sum(
            lax.dot_general(
                g_buf[(h,) + index + (slice(None), pl.ds(low, width))].reshape(256, width),
                down_out[:, pl.ds(h * HALF + low, width)], (((1,), (1,)), ((), ())),
                preferred_element_type=jnp.float32,
            )
            for h in range(2)
        ).reshape(4, 4, 16, FU)
        grad_hidden[index] = grad_hidden[index] + value

    def down_part(p, gs, h):
        low, _, high = OUT_PARTS[p]
        width = high - low
        groups = [place.group(p, ROWS_OUT[g]) for g in gs]
        lhs = jnp.concatenate([hidden[i + (slice(None), slice(None))].reshape(256, FU) for i in groups], axis=0)
        rhs = jnp.concatenate(
            [g_buf[(h,) + i + (slice(None), pl.ds(low, width))].reshape(256, width) for i in groups], axis=0
        )
        value = lax.dot_general(lhs, rhs, (((0,), (0,)), ((), ())), preferred_element_type=jnp.float32)
        return pl.ds(h * HALF + low, width), value

    outs = Gather(place, g_buf, OUT_PARTS, sems[9:14])

    def back(g):
        for p in range(3):
            outs.take_across(p, g)
            backward(p, g)

    outs.send_blocks()
    ins.finish()
    outs.send_rows()
    red.finish()
    outs.take_row(1)
    outs.take_row(2)
    outs.take_row(3)
    outs.cross(0)

    @pl.loop(0, 4)
    def _(x):
        row_scale, _ = facts(x)
        gate, up = acc_gate[x].reshape(256, FU), acc_up[x].reshape(256, FU)
        sigma = jax.nn.sigmoid(gate)
        acc_gate[x] = (row_scale * up * sigma * (1.0 + gate * (1.0 - sigma))).reshape(4, 4, 16, FU)
        acc_up[x] = (row_scale * gate * sigma).reshape(4, 4, 16, FU)

    outs.pass_on(0)
    outs.pass_on(1)
    back(0)
    outs.pass_on(2)
    outs.pass_on(3)
    outs.cross(1)
    outs.cross(2)
    back(1)
    back(2)
    for p in range(3):
        for h in range(2):
            cols, value = down_part(p, (0, 1, 2), h)
            down_sum[:, cols] = value
    for r in range(4):
        outs.take_far(r)
    outs.cross(3)
    outs.finish()
    back(3)

    @pl.loop(0, 4)
    def _(x):
        grad = grad_hidden[x].reshape(256, FU)
        cols = pl.ds(pl.multiple_of(x * 256, 256), 256)
        pre_t[pl.ds(0, FU), cols] = (grad * acc_gate[x].reshape(256, FU)).T.astype(jnp.bfloat16)
        pre_t[pl.ds(FU, FU), cols] = (grad * acc_up[x].reshape(256, FU)).T.astype(jnp.bfloat16)

    for p in range(3):
        for h in range(2):
            cols, value = down_part(p, (3,), h)
            down_out[:, cols] = (down_sum[:, cols] + value).astype(jnp.bfloat16)
    for h in range(2):
        for t in range(HALF // 512):
            cols = pl.ds(t * 512, 512)
            spot = pl.ds(h * HALF + t * 512, 512)
            value = jnp.dot(
                pre_t[...], x_buf[h, :, :, :, :, cols].reshape(TOKENS, 512), preferred_element_type=jnp.float32
            )
            first_gain = h * 16 + t * 4
            gain = jnp.concatenate([sgain_ref[first_gain + i:first_gain + i + 1, :] for i in range(4)], axis=1)
            gate_out[:, spot] = (value[:FU] * gain).astype(jnp.bfloat16)
            up_out[:, spot] = (value[FU:] * gain).astype(jnp.bfloat16)


def step(tokens, ids, weights, tgain, sgain, eg, eu, ed, sg, su, sd):
    bf16, f32 = jnp.bfloat16, jnp.float32
    vmem, hbm = pl.BlockSpec(memory_space=pltpu.VMEM), pl.BlockSpec(memory_space=pl.ANY)
    return pl.pallas_call(
        step_kernel,
        out_shape=(pltpu.VMEM((FU, D), bf16),) * 3,
        in_specs=[vmem] * 5 + [hbm] * 6,
        out_specs=[vmem] * 3,
        scratch_shapes=[
            pltpu.VMEM((2, 4, 4, 4, 16, WIDE), bf16),
            pltpu.VMEM((2, 4, 4, 4, 16, HALF), bf16),
            pltpu.VMEM((2, 4, 4, 4, 16, HALF), bf16),
            pltpu.VMEM((4, 4, 4, 16, HALF), bf16),
            pltpu.VMEM((D, 2 * FE), bf16),
            pltpu.VMEM((512, D), bf16),
            pltpu.VMEM((4, 4, 4, 16, 2 * FE), f32),
            pltpu.VMEM((4, 4, 4, 16, FU), f32),
            pltpu.VMEM((4, 4, 4, 16, FU), f32),
            pltpu.VMEM((4, 4, 4, 16, FU), f32),
            pltpu.VMEM((4, 4, 4, 16, 512), bf16),
            pltpu.VMEM((4, 4, 4, 16, FU), bf16),
            pltpu.VMEM((FU, D), f32),
            pltpu.VMEM((2 * FU, TOKENS), bf16),
            pltpu.VMEM((2, 8, WIDE), f32),
            pltpu.VMEM((8, WIDE), f32),
        ]
        + [pltpu.VMEM((2, 3, 4, 4, 16, 384), bf16)] * 3
        + [
            pltpu.VMEM((3, 4, 16, HALF), bf16),
            pltpu.VMEM((3, 16, HALF), bf16),
            pltpu.SemaphoreType.DMA((5, 4)),
            pltpu.SemaphoreType.DMA((2,)),
        ]
        + GATHER_SEMS
        + REDUCE_SEMS
        + GATHER_SEMS,
        compiler_params=pltpu.CompilerParams(collective_id=0, has_side_effects=True, vmem_limit_bytes=57 << 20),
        name="distill",
    )(tokens, ids, weights, tgain, sgain, eg, eu, ed, sg, su, sd)


def body(
    tokens, teacher_gain, student_gain, expert_ids, route_weights,
    expert_gate, expert_up, expert_down, student_gate, student_up, student_down,
):
    gate, up, down = step(
        tokens, expert_ids, route_weights, teacher_gain.reshape(32, 128), student_gain.reshape(32, 128),
        expert_gate[0], expert_up[0], expert_down[0], student_gate.T, student_up.T, student_down,
    )
    return gate.T, up.T, down


def solution(mesh):
    everywhere = ("grp", "ep", "tp")
    in_specs = (
        P(everywhere, None),
        P(),
        P(),
        P(everywhere, None),
        P(everywhere, None),
        P(("grp", "ep"), None, "tp"),
        P(("grp", "ep"), None, "tp"),
        P(("grp", "ep"), "tp", None),
        P(None, ("ep", "tp")),
        P(None, ("ep", "tp")),
        P(("ep", "tp"), None),
    )
    out_specs = (P(None, ("ep", "tp")), P(None, ("ep", "tp")), P(("ep", "tp"), None))
    return jax.shard_map(body, mesh=mesh, in_specs=in_specs, out_specs=out_specs, check_vma=False)
```
